512 devices in a mesh: rep: 32 (over z, y_hi, core), fsdp: 16 (over x, y_lo).
Axes of the slice: x: 4, y: 8 (y_hi: 2, y_lo: 4; y = y_hi * 4 + y_lo), z: 8, core: 2. Of those that a mesh axis runs over, the one named last changes fastest.
Arguments:
- hidden: bfloat16 [32, 2048, 4096], P('rep', 'fsdp'), may hold values from -150 to 150
- gain: bfloat16 [32, 4096], P('rep'), may hold values from 0.25 to 1.75
- value_grad: bfloat16 [32, 2048, 512], P('rep', 'fsdp'), may hold values from -6 to 6
- value_weight: bfloat16 [32, 4096, 512], P('rep', 'fsdp'), may hold values from -0.09375 to 0.09375
- outer_delta: bfloat16 [32, 4096, 512], P('rep', 'fsdp'), may hold values from -6 to 6
- momentum: float32 [4096, 512], P('fsdp'), may hold values from -6 to 6
Outputs:
- values: bfloat16 [32, 2048, 512], P('rep', 'fsdp')
- value_weight_grad: bfloat16 [32, 4096, 512], P('rep', 'fsdp')
- hidden_grad: bfloat16 [32, 2048, 4096], P('rep', 'fsdp')
- new_momentum: float32 [4096, 512], P('fsdp')
- outer_step: float32 [4096, 512], P('fsdp')
The draws below stay inside these ranges and needn't reach their ends.
All inputs are finite; a program needn't handle non-finite values.
Results may differ from the reference program's by a relative error of at most 0.022.
Values may be sent and summed in bfloat16 or wider, within the bound.
A program may use at most 64 MiB of HBM per device.

```python
import math
import jax
import jax.numpy as jnp
from jax import lax

D = 4096
TOK_DEV = 128
KVW = 512
TOKENS = 2048
REPS = 32
N_FSDP = 16


def draw_hidden(key, part):
    key = jax.random.fold_in(key, 7)
    subkeys = jax.random.split(key, 3)
    spread = math.log(10.0)
    row_scale = jnp.exp(jax.random.uniform(subkeys[1], (REPS, TOKENS, 1), jnp.float32) * spread)
    col_scale = jnp.exp(jax.random.uniform(subkeys[2], (1, 1, D), jnp.float32) * spread)
    entries = jax.random.normal(subkeys[0], (REPS, TOKENS, D), jnp.float32)
    entries = jnp.clip(entries, -5.0, 5.0)
    return (0.3 * entries * row_scale * col_scale).astype(jnp.bfloat16)


def steps_of(rng, dims, pieces, low, largest):
    loudness, own = 1.0, jax.random.fold_in(rng, 6)
    for dim, shards_of in pieces:
        draws = jnp.exp(jax.random.uniform(jax.random.fold_in(own, dim), (shards_of,), jnp.float32, low / len(pieces), largest / len(pieces)))
        loudness = loudness * jnp.repeat(draws, dims[dim] // shards_of).reshape([-1 if axis == dim else 1 for axis in range(len(dims))])
    return loudness


def scatter_about(key, dims, deviation, reach, shards=(), kind=jnp.bfloat16):
    level = steps_of(key, dims, shards, -0.22, 0.18) if shards else 1.0
    array = jax.random.normal(key, dims, jnp.float32) * deviation * level
    return jnp.minimum(jnp.maximum(array, -reach), reach).astype(kind)


def setup_inputs(seed: int = 0) -> dict:
    arg_keys = jax.random.split(jax.random.key(seed), 7)
    return {
        "hidden": draw_hidden(jax.random.fold_in(arg_keys[6], 71), 0),
        "gain": jnp.clip(1.0 + 0.15 * jax.random.normal(arg_keys[1], (REPS, D), jnp.float32), 0.25, 1.75).astype(jnp.bfloat16),
        "value_grad": scatter_about(arg_keys[2], (REPS, TOKENS, KVW), 1.0, 6.0, ((0, 32), (1, 16))),
        "value_weight": scatter_about(arg_keys[3], (REPS, D, KVW), D ** -0.5, 0.09375, ((0, 32), (1, 16))),
        "outer_delta": scatter_about(arg_keys[4], (REPS, D, KVW), 1.0, 6.0, ((0, 32), (1, 16))),
        "momentum": scatter_about(arg_keys[5], (D, KVW), 1.0, 6.0, ((0, 16),), jnp.float32),
    }


EPSILON = 1e-05
MOMENT = 0.9
OUTER_RATE = 0.7

def one_replica(operands):
    hidden, gain, value_grad, value_weight = operands
    widened = hidden.astype(jnp.float32)
    inverse_rms = lax.rsqrt(lax.optimization_barrier(jnp.mean(widened * widened, axis=-1, keepdims=True)) + EPSILON)
    scaled = widened * inverse_rms
    gain_wide = gain.astype(jnp.float32)
    normed = (scaled * gain_wide).astype(jnp.bfloat16)
    values = jnp.dot(normed, value_weight, preferred_element_type=jnp.float32).astype(jnp.bfloat16)
    blocks_normed = normed.reshape(N_FSDP, TOK_DEV, D).astype(jnp.float32)
    blocks_grad = value_grad.reshape(N_FSDP, TOK_DEV, KVW).astype(jnp.float32)
    partials = jnp.einsum('ntd,ntv->ndv', blocks_normed, blocks_grad) / TOK_DEV
    rounded = lax.optimization_barrier(partials.astype(jnp.bfloat16))
    weight_grad = lax.optimization_barrier(jnp.sum(rounded.astype(jnp.float32), axis=0)).astype(jnp.bfloat16)
    normed_grad = jnp.dot(value_grad, value_weight.T, preferred_element_type=jnp.float32).astype(jnp.bfloat16)
    gated = normed_grad.astype(jnp.float32) * gain_wide
    centred = gated - scaled * lax.optimization_barrier(jnp.mean(gated * scaled, axis=-1, keepdims=True))
    hidden_grad = (inverse_rms * centred).astype(jnp.bfloat16)
    return (values, weight_grad, hidden_grad)

def reference(hidden, gain, value_grad, value_weight, outer_delta, momentum):
    values, weight_grad, hidden_grad = lax.map(one_replica, (hidden, gain, value_grad, value_weight))
    summed = lax.optimization_barrier(jnp.sum(outer_delta.astype(jnp.float32), axis=0))
    average = summed / REPS
    new_momentum = MOMENT * momentum + average
    outer_step = -OUTER_RATE * (average + MOMENT * new_momentum)
    return (values, weight_grad, hidden_grad, new_momentum, outer_step)
```

```python
import jax
import jax.numpy as jnp
from jax import lax
from jax.experimental import pallas as pl
from jax.experimental.pallas import tpu as pltpu
from jax.sharding import PartitionSpec as P

EPSILON = 1e-05
MOMENT = 0.9
OUTER_RATE = 0.7

TOK = 128
D = 4096
KV = 512
ROWS = 256
NX = 4
NY = 4
NZ = 8
GROUP = NX * TOK
SLICE = 16

MESH = pl.DeviceIdType.MESH
F32 = jnp.float32
BF16 = jnp.bfloat16


def exchange(
    hidden, gain, value_grad, weight, delta, momentum,
    hg_out, val_out, wg_out, nm_out, os_out,
    h_v, inv_v, row_v, n_send, n_buf, vg_buf, w_buf, ng_send, ng_buf,
    v_send, v_recv, wg_acc, wg_send, wg_recv,
    d_own, d_recv, p_send, z_recv, s_own, s_recv, avg, mom_v,
    local_sem, x_send, x_recv, n_ssem, n_rsem, g_ssem, g_rsem, v_ssem, v_rsem,
    w_ssem, w_rsem, r_ssem, r_rsem, c_ssem, c_rsem, z_ssem, z_rsem, a_ssem, a_rsem,
):
    rep = lax.axis_index("rep")
    fsdp = lax.axis_index("fsdp")
    i, j = fsdp // NY, fsdp % NY
    z, core = rep // 4, rep % 2
    high = j // 2
    mid = jnp.logical_or(j == 1, j == 2)
    outer = jnp.logical_not(mid)
    is_mid = high + j % 2 - 2 * high * (j % 2)

    def along_x(d):
        return (rep, ((i + d) % NX) * NY + j)

    def along_z(d):
        return (((z + d) % NZ) * 4 + rep % 4, fsdp)

    inward = (rep, i * NY + j + 1 - 2 * high)
    outward = (rep, i * NY + j - 1 + 2 * high)
    other_core = (rep + 1 - 2 * core, fsdp)
    other_half = (rep + 2 - 4 * ((rep // 2) % 2), fsdp)
    near = j + 1 - 2 * (j % 2)
    far_mid = 2 - high
    far_outer = 3 - 3 * high
    arrival = (j, near, far_mid, far_outer)
    order = (far_outer, far_mid, near, j)

    def remote(src, dst, ssem, rsem, device):
        return pltpu.make_async_remote_copy(
            src_ref=src, dst_ref=dst, send_sem=ssem, recv_sem=rsem,
            device_id=device, device_id_type=MESH,
        )

    barrier = pltpu.get_barrier_semaphore()

    def greet(device):
        pl.semaphore_signal(barrier, inc=1, device_id=device, device_id_type=MESH)

    for d in range(1, NX):
        greet(along_x(d))
    greet(inward)

    @pl.when(mid)
    def _():
        greet(outward)

    greet(other_core)
    greet(other_half)
    for d in range(1, NZ):
        greet(along_z(d))

    own_rows = pl.ds(pl.multiple_of(i * TOK, TOK), TOK)
    half_rows = lambda h: pl.ds(pl.multiple_of(h * TOK, TOK), TOK)
    slice_rows = lambda s: pl.ds(pl.multiple_of(s * SLICE, SLICE), SLICE)

    loads = [
        pltpu.make_async_copy(hidden, h_v, local_sem.at[0]),
        pltpu.make_async_copy(value_grad, vg_buf.at[own_rows], local_sem.at[1]),
        pltpu.make_async_copy(weight, w_buf.at[j], local_sem.at[2]),
        pltpu.make_async_copy(delta.at[half_rows(core)], d_own, local_sem.at[3]),
        pltpu.make_async_copy(momentum, mom_v, local_sem.at[4]),
    ]
    for load in loads:
        load.start()

    pl.semaphore_wait(barrier, 13 + is_mid)

    vg_copies = [
        remote(value_grad, vg_buf.at[own_rows], x_send.at[d], x_recv.at[d], along_x(d))
        for d in range(1, NX)
    ]
    for copy in vg_copies:
        copy.start()
    w_first = remote(weight, w_buf.at[j], w_ssem.at[0], w_rsem.at[j], inward)
    w_second = remote(weight, w_buf.at[j], w_ssem.at[1], w_rsem.at[j], outward)
    w_first.start()

    @pl.when(mid)
    def _():
        w_second.start()

    core_half = remote(
        delta.at[half_rows(1 - core)], d_recv, c_ssem.at[0], c_rsem.at[0], other_core
    )
    core_half.start()

    loads[0].wait()

    def columns(f):
        return pl.ds(pl.multiple_of(f * ROWS, ROWS), ROWS)

    def add_square(f, total):
        block = h_v[:, columns(f)].astype(F32)
        return total + block * block

    squares = lax.fori_loop(0, 16, add_square, jnp.zeros((TOK, ROWS), F32))
    inv_v[...] = lax.rsqrt(jnp.sum(squares, axis=-1, keepdims=True) / D + EPSILON)

    @pl.loop(0, 16)
    def _(f):
        scaled = h_v[:, columns(f)].astype(F32) * inv_v[...]
        n_send[f] = (scaled * gain[:, columns(f)].astype(F32)).astype(BF16)

    n_copies = []
    for n, block in enumerate(order):
        for d in (1, 3, 2):
            copy = remote(
                n_send.at[((i + d) % NX) * NY + block], n_buf.at[block, own_rows],
                n_ssem.at[n, d], n_rsem.at[n, d], along_x(d),
            )
            copy.start()
            n_copies.append(copy)
    for block in range(NY):
        n_buf[block, own_rows] = n_send[i * NY + block]

    loads[3].wait()
    core_half.wait_recv()
    p_send[...] = (d_own[...].astype(F32) + d_recv[...].astype(F32)).astype(BF16)
    z_copies = [
        remote(
            p_send.at[slice_rows((z + d) % NZ)], z_recv.at[d - 1],
            z_ssem.at[d], z_rsem.at[d], along_z(d),
        )
        for d in range(1, NZ)
    ]
    for copy in z_copies:
        copy.start()

    def w_arrive(n):
        block = arrival[n]
        remote(
            w_buf.at[block], w_buf.at[block], w_ssem.at[0], w_rsem.at[block], inward
        ).wait_recv()

    def w_forward(n):
        block = arrival[n]
        return remote(
            w_buf.at[block], w_buf.at[block], w_ssem.at[n + 1], w_rsem.at[block],
            inward if n == 1 else outward,
        )

    def take_weight(n):
        w_arrive(n)

        @pl.when(mid)
        def _():
            w_forward(n).start()

    g_copies = []

    def send_grad(n):
        block = arrival[n]
        ng_send[n] = lax.dot_general(
            vg_buf[...], w_buf[block], (((1,), (1,)), ((), ())), preferred_element_type=F32
        ).astype(BF16)
        for d in (1, 3, 2):
            copy = remote(
                ng_send.at[n, pl.ds(pl.multiple_of(((i + d) % NX) * TOK, TOK), TOK)],
                ng_buf.at[i * NY + block], g_ssem.at[n, d], g_rsem.at[n, d], along_x(d),
            )
            copy.start()
            g_copies.append(copy)
        ng_buf[i * NY + block] = ng_send[n, own_rows]

    def make_weight_grad(n):
        for d in range(1, NX):
            n_copies[3 * n + (0, 0, 2, 1)[d]].wait_recv()
        block = order[n]
        wg_acc[block] = lax.dot_general(
            n_buf[block], vg_buf[...], (((0,), (0,)), ((), ())), preferred_element_type=F32
        ) * (1.0 / TOK)

    def first_hop(n):
        return remote(
            wg_send.at[order[n]], wg_recv.at[n], r_ssem.at[n], r_rsem.at[n], inward
        )

    def start_chain(n):
        @pl.when(outer)
        def _():
            wg_send[order[n]] = wg_acc[order[n]].astype(BF16)
            first_hop(n).start()

    def next_hop(slot):
        block, target, device = (
            (far_outer, 3, inward), (far_mid, 4, inward), None, (near, 3, outward),
        )[slot]
        return block, remote(
            wg_send.at[block], wg_recv.at[target], r_ssem.at[slot], r_rsem.at[target], device
        )

    def r_arrive(slot):
        remote(
            wg_recv.at[slot], wg_recv.at[slot], r_ssem.at[0], r_rsem.at[slot], inward
        ).wait_recv()

    def pass_on(slot):
        @pl.when(mid)
        def _():
            block, copy = next_hop(slot)
            r_arrive(slot)
            wg_send[block] = (wg_acc[block] + wg_recv[slot].astype(F32)).astype(BF16)
            copy.start()

    loads[1].wait()
    loads[2].wait()
    for copy in vg_copies:
        copy.wait_recv()
    send_grad(0)
    take_weight(1)

    for copy in z_copies:
        copy.wait_recv()
    total = (
        d_own[slice_rows(z)].astype(F32) + d_recv[slice_rows(z)].astype(F32)
    )
    for d in range(NZ - 1):
        total = total + z_recv[d].astype(F32)
    s_own[...] = total
    half_copy = remote(s_own, s_recv, c_ssem.at[1], c_rsem.at[1], other_half)
    half_copy.start()

    make_weight_grad(0)
    start_chain(0)
    send_grad(1)
    take_weight(2)
    make_weight_grad(1)
    start_chain(1)
    send_grad(2)

    half_copy.wait_recv()
    half_copy.wait_send()
    avg[core, slice_rows(z)] = (s_own[...] + s_recv[...]) / 32.0
    a_copies = [
        remote(
            avg.at[core, slice_rows(z)], avg.at[core, slice_rows(z)],
            a_ssem.at[d], a_rsem.at[d], along_z(d),
        )
        for d in range(1, NZ)
    ]
    for copy in a_copies:
        copy.start()

    make_weight_grad(2)
    start_chain(2)
    pass_on(0)
    take_weight(3)
    send_grad(3)
    make_weight_grad(3)

    v_acc = jnp.dot(n_buf[0], w_buf[0], preferred_element_type=F32)
    for block in range(1, NY):
        v_acc = v_acc + jnp.dot(n_buf[block], w_buf[block], preferred_element_type=F32)
    v_send[...] = v_acc.astype(BF16)
    v_copies = []
    for d in (1, 3, 2):
        copy = remote(
            v_send.at[pl.ds(pl.multiple_of(((i + d) % NX) * TOK, TOK), TOK)],
            v_recv.at[d - 1], v_ssem.at[d], v_rsem.at[d], along_x(d),
        )
        copy.start()
        v_copies.append(copy)

    for copy in a_copies:
        copy.wait_recv()
    core_full = remote(avg.at[core], avg.at[core], c_ssem.at[2], c_rsem.at[2], other_core)
    core_full.start()

    pass_on(3)
    pass_on(1)

    core_back = remote(
        avg.at[1 - core], avg.at[1 - core], c_ssem.at[2], c_rsem.at[2], other_core
    )
    core_back.wait_recv()
    loads[4].wait()
    for h in range(2):
        rows = pl.ds(h * TOK, TOK)
        new_momentum = MOMENT * mom_v[rows] + avg[h]
        nm_out[rows] = new_momentum
        os_out[rows] = -OUTER_RATE * (avg[h] + MOMENT * new_momentum)

    def gated_scaled(f):
        scaled = h_v[:, columns(f)].astype(F32) * inv_v[...]
        gated = ng_buf[f].astype(F32) * gain[:, columns(f)].astype(F32)
        return gated, scaled

    row_v[...] = jnp.zeros_like(row_v)

    def add_rows(f):
        gated, scaled = gated_scaled(f)
        row_v[...] += gated * scaled

    for n in range(NY):
        add_rows(i * NY + arrival[n])
    for n in range(NY):
        for d in range(1, NX):
            g_copies[3 * n + (0, 0, 2, 1)[d]].wait_recv()
            add_rows(((i + NX - d) % NX) * NY + arrival[n])
    mean = jnp.sum(row_v[...], axis=-1, keepdims=True) / D

    @pl.loop(0, 16)
    def _(f):
        gated, scaled = gated_scaled(f)
        hg_out[:, columns(f)] = (inv_v[...] * (gated - scaled * mean)).astype(BF16)

    @pl.when(outer)
    def _():
        r_arrive(3)
        wg_out[...] = (wg_acc[j] + wg_recv[3].astype(F32)).astype(BF16)

    @pl.when(mid)
    def _():
        r_arrive(2)
        r_arrive(4)
        wg_out[...] = (
            wg_acc[j] + wg_recv[2].astype(F32) + wg_recv[4].astype(F32)
        ).astype(BF16)

    value_sum = v_send[own_rows].astype(F32)
    for copy in v_copies:
        copy.wait_recv()
    for d in range(NX - 1):
        value_sum = value_sum + v_recv[d].astype(F32)
    val_out[...] = value_sum.astype(BF16)

    for copy in (*vg_copies, w_first, core_half, *n_copies, *z_copies, *g_copies, *a_copies):
        copy.wait_send()
    for copy in (*v_copies, core_full):
        copy.wait_send()

    @pl.when(mid)
    def _():
        w_second.wait_send()
        for n in range(1, NY):
            w_forward(n).wait_send()
        for slot in (0, 1, 3):
            next_hop(slot)[1].wait_send()

    @pl.when(outer)
    def _():
        for n in range(3):
            first_hop(n).wait_send()


def per_device(hidden, gain, value_grad, value_weight, outer_delta, momentum):
    anywhere = pl.BlockSpec(memory_space=pl.ANY)
    vmem = pl.BlockSpec(memory_space=pltpu.VMEM)
    dma = pltpu.SemaphoreType.DMA
    outs = pl.pallas_call(
        exchange,
        out_shape=(
            jax.ShapeDtypeStruct((TOK, D), BF16),
            jax.ShapeDtypeStruct((TOK, KV), BF16),
            jax.ShapeDtypeStruct((ROWS, KV), BF16),
            jax.ShapeDtypeStruct((ROWS, KV), F32),
            jax.ShapeDtypeStruct((ROWS, KV), F32),
        ),
        in_specs=[anywhere, vmem, anywhere, anywhere, anywhere, anywhere],
        out_specs=[vmem] * 5,
        scratch_shapes=[
            pltpu.VMEM((TOK, D), BF16),
            pltpu.VMEM((TOK, 1), F32),
            pltpu.VMEM((TOK, ROWS), F32),
            pltpu.VMEM((16, TOK, ROWS), BF16),
            pltpu.VMEM((NY, GROUP, ROWS), BF16),
            pltpu.VMEM((GROUP, KV), BF16),
            pltpu.VMEM((NY, ROWS, KV), BF16),
            pltpu.VMEM((NY, GROUP, ROWS), BF16),
            pltpu.VMEM((16, TOK, ROWS), BF16),
            pltpu.VMEM((GROUP, KV), BF16),
            pltpu.VMEM((NX - 1, TOK, KV), BF16),
            pltpu.VMEM((NY, ROWS, KV), F32),
            pltpu.VMEM((NY, ROWS, KV), BF16),
            pltpu.VMEM((5, ROWS, KV), BF16),
            pltpu.VMEM((TOK, KV), BF16),
            pltpu.VMEM((TOK, KV), BF16),
            pltpu.VMEM((TOK, KV), BF16),
            pltpu.VMEM((NZ - 1, SLICE, KV), BF16),
            pltpu.VMEM((SLICE, KV), F32),
            pltpu.VMEM((SLICE, KV), F32),
            pltpu.VMEM((2, TOK, KV), F32),
            pltpu.VMEM((ROWS, KV), F32),
            dma((5,)),
            dma((NX,)), dma((NX,)),
            dma((NY, NX)), dma((NY, NX)),
            dma((NY, NX)), dma((NY, NX)),
            dma((NX,)), dma((NX,)),
            dma((5,)), dma((NY,)),
            dma((5,)), dma((5,)),
            dma((3,)), dma((3,)),
            dma((NZ,)), dma((NZ,)),
            dma((NZ,)), dma((NZ,)),
        ],
        compiler_params=pltpu.CompilerParams(
            collective_id=0, has_side_effects=True, vmem_limit_bytes=40 * 1024 * 1024
        ),
    )(hidden[0], gain, value_grad[0], value_weight[0], outer_delta[0], momentum)
    hidden_grad, values, weight_grad, new_momentum, outer_step = outs
    return (values[None], weight_grad[None], hidden_grad[None], new_momentum, outer_step)


def solution(mesh):
    in_specs = (
        P("rep", "fsdp", None),
        P("rep", None),
        P("rep", "fsdp", None),
        P("rep", "fsdp", None),
        P("rep", "fsdp", None),
        P("fsdp", None),
    )
    out_specs = (
        P("rep", "fsdp", None),
        P("rep", "fsdp", None),
        P("rep", "fsdp", None),
        P("fsdp", None),
        P("fsdp", None),
    )
    return jax.shard_map(
        per_device, mesh=mesh, in_specs=in_specs, out_specs=out_specs, check_vma=False
    )
```

```python
import jax
import jax.numpy as jnp
from jax import lax
from jax.experimental import pallas as pl
from jax.experimental.pallas import tpu as pltpu
from jax.sharding import PartitionSpec as P

EPSILON = 1e-05
MOMENT = 0.9
OUTER_RATE = 0.7

TOK = 128
D = 4096
KV = 512
ROWS = 256
NX = 4
NY = 4
NZ = 8
GROUP = NX * TOK
SLICE = 16

MESH = pl.DeviceIdType.MESH
F32 = jnp.float32
BF16 = jnp.bfloat16


def exchange(
    hidden, gain, value_grad, weight, delta, momentum,
    hg_out, val_out, wg_out, nm_out, os_out,
    h_v, inv_v, row_v, n_send, n_buf, vg_buf, w_buf, ng_send, ng_buf,
    v_send, v_recv, wg_acc, wg_send, wg_recv,
    d_own, d_recv, p_send, z_recv, s_own, s_recv, avg, mom_v,
    local_sem, x_send, x_recv, n_ssem, n_rsem, g_ssem, g_rsem, v_ssem, v_rsem,
    w_ssem, w_rsem, r_ssem, r_rsem, c_ssem, c_rsem, z_ssem, z_rsem, a_ssem, a_rsem,
):
    rep = lax.axis_index("rep")
    fsdp = lax.axis_index("fsdp")
    i, j = fsdp // NY, fsdp % NY
    z, core = rep // 4, rep % 2
    high = j // 2
    mid = jnp.logical_or(j == 1, j == 2)
    outer = jnp.logical_not(mid)
    is_mid = high + j % 2 - 2 * high * (j % 2)

    def along_x(d):
        return (rep, ((i + d) % NX) * NY + j)

    def along_z(d):
        return (((z + d) % NZ) * 4 + rep % 4, fsdp)

    inward = (rep, i * NY + j + 1 - 2 * high)
    outward = (rep, i * NY + j - 1 + 2 * high)
    other_core = (rep + 1 - 2 * core, fsdp)
    other_half = (rep + 2 - 4 * ((rep // 2) % 2), fsdp)
    near = j + 1 - 2 * (j % 2)
    far_mid = 2 - high
    far_outer = 3 - 3 * high
    arrival = (j, near, far_mid, far_outer)
    order = (far_outer, far_mid, near, j)

    def remote(src, dst, ssem, rsem, device):
        return pltpu.make_async_remote_copy(
            src_ref=src, dst_ref=dst, send_sem=ssem, recv_sem=rsem,
            device_id=device, device_id_type=MESH,
        )

    barrier = pltpu.get_barrier_semaphore()

    def greet(device):
        pl.semaphore_signal(barrier, inc=1, device_id=device, device_id_type=MESH)

    for d in range(1, NX):
        greet(along_x(d))
    greet(inward)

    @pl.when(mid)
    def _():
        greet(outward)

    greet(other_core)
    greet(other_half)
    for d in range(1, NZ):
        greet(along_z(d))

    own_rows = pl.ds(pl.multiple_of(i * TOK, TOK), TOK)
    half_rows = lambda h: pl.ds(pl.multiple_of(h * TOK, TOK), TOK)
    slice_rows = lambda s: pl.ds(pl.multiple_of(s * SLICE, SLICE), SLICE)

    loads = [
        pltpu.make_async_copy(hidden, h_v, local_sem.at[0]),
        pltpu.make_async_copy(value_grad, vg_buf.at[own_rows], local_sem.at[1]),
        pltpu.make_async_copy(weight, w_buf.at[j], local_sem.at[2]),
        pltpu.make_async_copy(delta.at[half_rows(core)], d_own, local_sem.at[3]),
        pltpu.make_async_copy(momentum, mom_v, local_sem.at[4]),
    ]
    for load in loads:
        load.start()

    pl.semaphore_wait(barrier, 13 + is_mid)

    vg_copies = [
        remote(value_grad, vg_buf.at[own_rows], x_send.at[d], x_recv.at[d], along_x(d))
        for d in range(1, NX)
    ]
    for copy in vg_copies:
        copy.start()
    w_first = remote(weight, w_buf.at[j], w_ssem.at[0], w_rsem.at[j], inward)
    w_second = remote(weight, w_buf.at[j], w_ssem.at[1], w_rsem.at[j], outward)
    w_first.start()

    @pl.when(mid)
    def _():
        w_second.start()

    core_half = remote(
        delta.at[half_rows(1 - core)], d_recv, c_ssem.at[0], c_rsem.at[0], other_core
    )
    core_half.start()

    loads[0].wait()

    def columns(f):
        return pl.ds(pl.multiple_of(f * ROWS, ROWS), ROWS)

    def add_square(f, total):
        block = h_v[:, columns(f)].astype(F32)
        return total + block * block

    squares = lax.fori_loop(0, 16, add_square, jnp.zeros((TOK, ROWS), F32))
    inv_v[...] = lax.rsqrt(jnp.sum(squares, axis=-1, keepdims=True) / D + EPSILON)

    @pl.loop(0, 16)
    def _(f):
        scaled = h_v[:, columns(f)].astype(F32) * inv_v[...]
        n_send[f] = (scaled * gain[:, columns(f)].astype(F32)).astype(BF16)

    n_copies = []
    for n, block in enumerate(order):
        for d in (1, 3, 2):
            copy = remote(
                n_send.at[((i + d) % NX) * NY + block], n_buf.at[block, own_rows],
                n_ssem.at[n, d], n_rsem.at[n, d], along_x(d),
            )
            copy.start()
            n_copies.append(copy)
    for block in range(NY):
        n_buf[block, own_rows] = n_send[i * NY + block]

    loads[3].wait()
    core_half.wait_recv()
    p_send[...] = (d_own[...].astype(F32) + d_recv[...].astype(F32)).astype(BF16)
    z_copies = [
        remote(
            p_send.at[slice_rows((z + d) % NZ)], z_recv.at[d - 1],
            z_ssem.at[d], z_rsem.at[d], along_z(d),
        )
        for d in range(1, NZ)
    ]
    for copy in z_copies:
        copy.start()

    def w_arrive(n):
        block = arrival[n]
        remote(
            w_buf.at[block], w_buf.at[block], w_ssem.at[0], w_rsem.at[block], inward
        ).wait_recv()

    def w_forward(n):
        block = arrival[n]
        return remote(
            w_buf.at[block], w_buf.at[block], w_ssem.at[n + 1], w_rsem.at[block],
            inward if n == 1 else outward,
        )

    def take_weight(n):
        w_arrive(n)

        @pl.when(mid)
        def _():
            w_forward(n).start()

    g_copies = []

    def send_grad(n):
        block = arrival[n]
        ng_send[n] = lax.dot_general(
            vg_buf[...], w_buf[block], (((1,), (1,)), ((), ())), preferred_element_type=F32
        ).astype(BF16)
        for d in (1, 3, 2):
            copy = remote(
                ng_send.at[n, pl.ds(pl.multiple_of(((i + d) % NX) * TOK, TOK), TOK)],
                ng_buf.at[i * NY + block], g_ssem.at[n, d], g_rsem.at[n, d], along_x(d),
            )
            copy.start()
            g_copies.append(copy)
        ng_buf[i * NY + block] = ng_send[n, own_rows]

    def make_weight_grad(n):
        for d in range(1, NX):
            n_copies[3 * n + (0, 0, 2, 1)[d]].wait_recv()
        block = order[n]
        wg_acc[block] = lax.dot_general(
            n_buf[block], vg_buf[...], (((0,), (0,)), ((), ())), preferred_element_type=F32
        ) * (1.0 / TOK)

    def first_hop(n):
        return remote(
            wg_send.at[order[n]], wg_recv.at[n], r_ssem.at[n], r_rsem.at[n], inward
        )

    def start_chain(n):
        @pl.when(outer)
        def _():
            wg_send[order[n]] = wg_acc[order[n]].astype(BF16)
            first_hop(n).start()

    def next_hop(slot):
        block, target, device = (
            (far_outer, 3, inward), (far_mid, 4, inward), None, (near, 3, outward),
        )[slot]
        return block, remote(
            wg_send.at[block], wg_recv.at[target], r_ssem.at[slot], r_rsem.at[target], device
        )

    def r_arrive(slot):
        remote(
            wg_recv.at[slot], wg_recv.at[slot], r_ssem.at[0], r_rsem.at[slot], inward
        ).wait_recv()

    def pass_on(slot):
        @pl.when(mid)
        def _():
            block, copy = next_hop(slot)
            r_arrive(slot)
            wg_send[block] = (wg_acc[block] + wg_recv[slot].astype(F32)).astype(BF16)
            copy.start()

    loads[1].wait()
    loads[2].wait()
    for copy in vg_copies:
        copy.wait_recv()
    send_grad(0)
    take_weight(1)

    for copy in z_copies:
        copy.wait_recv()
    total = (
        d_own[slice_rows(z)].astype(F32) + d_recv[slice_rows(z)].astype(F32)
    )
    for d in range(NZ - 1):
        total = total + z_recv[d].astype(F32)
    s_own[...] = total
    half_copy = remote(s_own, s_recv, c_ssem.at[1], c_rsem.at[1], other_half)
    half_copy.start()

    make_weight_grad(0)
    start_chain(0)
    send_grad(1)
    take_weight(2)
    make_weight_grad(1)
    start_chain(1)
    send_grad(2)

    half_copy.wait_recv()
    half_copy.wait_send()
    avg[core, slice_rows(z)] = (s_own[...] + s_recv[...]) / 32.0
    a_copies = [
        remote(
            avg.at[core, slice_rows(z)], avg.at[core, slice_rows(z)],
            a_ssem.at[d], a_rsem.at[d], along_z(d),
        )
        for d in range(1, NZ)
    ]
    for copy in a_copies:
        copy.start()

    make_weight_grad(2)
    start_chain(2)
    pass_on(0)
    take_weight(3)
    send_grad(3)
    make_weight_grad(3)

    v_acc = jnp.dot(n_buf[0], w_buf[0], preferred_element_type=F32)
    for block in range(1, NY):
        v_acc = v_acc + jnp.dot(n_buf[block], w_buf[block], preferred_element_type=F32)
    v_send[...] = v_acc.astype(BF16)
    v_copies = []
    for d in (1, 3, 2):
        copy = remote(
            v_send.at[pl.ds(pl.multiple_of(((i + d) % NX) * TOK, TOK), TOK)],
            v_recv.at[d - 1], v_ssem.at[d], v_rsem.at[d], along_x(d),
        )
        copy.start()
        v_copies.append(copy)

    for copy in a_copies:
        copy.wait_recv()
    core_full = remote(avg.at[core], avg.at[core], c_ssem.at[2], c_rsem.at[2], other_core)
    core_full.start()

    pass_on(3)
    pass_on(1)

    core_back = remote(
        avg.at[1 - core], avg.at[1 - core], c_ssem.at[2], c_rsem.at[2], other_core
    )
    core_back.wait_recv()
    loads[4].wait()
    for h in range(2):
        rows = pl.ds(h * TOK, TOK)
        new_momentum = MOMENT * mom_v[rows] + avg[h]
        nm_out[rows] = new_momentum
        os_out[rows] = -OUTER_RATE * (avg[h] + MOMENT * new_momentum)

    def gated_scaled(f):
        scaled = h_v[:, columns(f)].astype(F32) * inv_v[...]
        gated = ng_buf[f].astype(F32) * gain[:, columns(f)].astype(F32)
        return gated, scaled

    row_v[...] = jnp.zeros_like(row_v)

    def add_rows(f):
        gated, scaled = gated_scaled(f)
        row_v[...] += gated * scaled

    for n in range(NY):
        add_rows(i * NY + arrival[n])
    for n in range(NY):
        for d in range(1, NX):
            g_copies[3 * n + (0, 0, 2, 1)[d]].wait_recv()
            add_rows(((i + NX - d) % NX) * NY + arrival[n])
    mean = jnp.sum(row_v[...], axis=-1, keepdims=True) / D

    @pl.loop(0, 16)
    def _(f):
        gated, scaled = gated_scaled(f)
        hg_out[:, columns(f)] = (inv_v[...] * (gated - scaled * mean)).astype(BF16)

    @pl.when(outer)
    def _():
        r_arrive(3)
        wg_out[...] = (wg_acc[j] + wg_recv[3].astype(F32)).astype(BF16)

    @pl.when(mid)
    def _():
        r_arrive(2)
        r_arrive(4)
        wg_out[...] = (
            wg_acc[j] + wg_recv[2].astype(F32) + wg_recv[4].astype(F32)
        ).astype(BF16)

    value_sum = v_send[own_rows].astype(F32)
    for copy in v_copies:
        copy.wait_recv()
    for d in range(NX - 1):
        value_sum = value_sum + v_recv[d].astype(F32)
    val_out[...] = value_sum.astype(BF16)

    for copy in (*vg_copies, w_first, core_half, *n_copies, *z_copies, *g_copies, *a_copies):
        copy.wait_send()
    for copy in (*v_copies, core_full):
        copy.wait_send()

    @pl.when(mid)
    def _():
        w_second.wait_send()
        for n in range(1, NY):
            w_forward(n).wait_send()
        for slot in (0, 1, 3):
            next_hop(slot)[1].wait_send()

    @pl.when(outer)
    def _():
        for n in range(3):
            first_hop(n).wait_send()


def store(*refs):
    sems = refs[-1]
    copies = [
        pltpu.make_async_copy(refs[k], refs[5 + k], sems.at[k]) for k in range(5)
    ]
    for copy in copies:
        copy.start()
    for copy in copies:
        copy.wait()


def per_device(hidden, gain, value_grad, value_weight, outer_delta, momentum):
    anywhere = pl.BlockSpec(memory_space=pl.ANY)
    vmem = pl.BlockSpec(memory_space=pltpu.VMEM)
    dma = pltpu.SemaphoreType.DMA
    shapes = (
        jax.ShapeDtypeStruct((TOK, D), BF16),
        jax.ShapeDtypeStruct((TOK, KV), BF16),
        jax.ShapeDtypeStruct((ROWS, KV), BF16),
        jax.ShapeDtypeStruct((ROWS, KV), F32),
        jax.ShapeDtypeStruct((ROWS, KV), F32),
    )
    outs = pl.pallas_call(
        exchange,
        out_shape=shapes,
        in_specs=[anywhere, vmem, anywhere, anywhere, anywhere, anywhere],
        out_specs=[vmem] * 5,
        scratch_shapes=[
            pltpu.VMEM((TOK, D), BF16),
            pltpu.VMEM((TOK, 1), F32),
            pltpu.VMEM((TOK, ROWS), F32),
            pltpu.VMEM((16, TOK, ROWS), BF16),
            pltpu.VMEM((NY, GROUP, ROWS), BF16),
            pltpu.VMEM((GROUP, KV), BF16),
            pltpu.VMEM((NY, ROWS, KV), BF16),
            pltpu.VMEM((NY, GROUP, ROWS), BF16),
            pltpu.VMEM((16, TOK, ROWS), BF16),
            pltpu.VMEM((GROUP, KV), BF16),
            pltpu.VMEM((NX - 1, TOK, KV), BF16),
            pltpu.VMEM((NY, ROWS, KV), F32),
            pltpu.VMEM((NY, ROWS, KV), BF16),
            pltpu.VMEM((5, ROWS, KV), BF16),
            pltpu.VMEM((TOK, KV), BF16),
            pltpu.VMEM((TOK, KV), BF16),
            pltpu.VMEM((TOK, KV), BF16),
            pltpu.VMEM((NZ - 1, SLICE, KV), BF16),
            pltpu.VMEM((SLICE, KV), F32),
            pltpu.VMEM((SLICE, KV), F32),
            pltpu.VMEM((2, TOK, KV), F32),
            pltpu.VMEM((ROWS, KV), F32),
            dma((5,)),
            dma((NX,)), dma((NX,)),
            dma((NY, NX)), dma((NY, NX)),
            dma((NY, NX)), dma((NY, NX)),
            dma((NX,)), dma((NX,)),
            dma((5,)), dma((NY,)),
            dma((5,)), dma((5,)),
            dma((3,)), dma((3,)),
            dma((NZ,)), dma((NZ,)),
            dma((NZ,)), dma((NZ,)),
        ],
        compiler_params=pltpu.CompilerParams(
            collective_id=0, has_side_effects=True, vmem_limit_bytes=40 * 1024 * 1024
        ),
    )(*[pltpu.with_memory_space_constraint(a, pltpu.HBM) for a in (hidden[0], gain, value_grad[0], value_weight[0], outer_delta[0], momentum)])
    hidden_grad, values, weight_grad, new_momentum, outer_step = pl.pallas_call(
        store,
        out_shape=shapes,
        in_specs=[anywhere] * 5,
        out_specs=[anywhere] * 5,
        scratch_shapes=[dma((5,))],
        compiler_params=pltpu.CompilerParams(vmem_limit_bytes=1024 * 1024),
    )(*outs)
    return (values[None], weight_grad[None], hidden_grad[None], new_momentum, outer_step)


def solution(mesh):
    in_specs = (
        P("rep", "fsdp", None),
        P("rep", None),
        P("rep", "fsdp", None),
        P("rep", "fsdp", None),
        P("rep", "fsdp", None),
        P("fsdp", None),
    )
    out_specs = (
        P("rep", "fsdp", None),
        P("rep", "fsdp", None),
        P("rep", "fsdp", None),
        P("fsdp", None),
        P("fsdp", None),
    )
    return jax.shard_map(
        per_device, mesh=mesh, in_specs=in_specs, out_specs=out_specs, check_vma=False
    )
```

```python
import jax
import jax.numpy as jnp
from jax import lax
from jax.experimental import pallas as pl
from jax.experimental.pallas import tpu as pltpu
from jax.sharding import PartitionSpec as P

EPSILON = 1e-05
MOMENT = 0.9
OUTER_RATE = 0.7

TOK = 128
D = 4096
KV = 512
ROWS = 256
NX = 4
NY = 4
NZ = 8
GROUP = NX * TOK
SLICE = 16

MESH = pl.DeviceIdType.MESH
F32 = jnp.float32
BF16 = jnp.bfloat16


def exchange(
    hidden, gain, value_grad, weight, delta, momentum,
    hg_out, val_out, wg_out, nm_out, os_out,
    h_v, inv_v, row_v, n_send, n_buf, vg_buf, w_buf, ng_send, ng_buf,
    v_send, v_recv, wg_acc, wg_send, wg_recv,
    d_own, d_recv, q_send, q_recv, p_send, z_recv, avg, mom_v,
    local_sem, x_send, x_recv, n_ssem, n_rsem, g_ssem, g_rsem, v_ssem, v_rsem,
    w_ssem, w_rsem, r_ssem, r_rsem, c_ssem, c_rsem, z_ssem, z_rsem, a_ssem, a_rsem,
    below_sem, above_sem,
):
    rep = lax.axis_index("rep")
    fsdp = lax.axis_index("fsdp")
    i, j = fsdp // NY, fsdp % NY
    z, core = rep // 4, rep % 2
    high = j // 2
    mid = jnp.logical_or(j == 1, j == 2)
    outer = jnp.logical_not(mid)
    is_mid = high + j % 2 - 2 * high * (j % 2)

    def along_x(d):
        return (rep, ((i + d) % NX) * NY + j)

    def along_z(d):
        return (((z + d) % NZ) * 4 + rep % 4, fsdp)

    inward = (rep, i * NY + j + 1 - 2 * high)
    outward = (rep, i * NY + j - 1 + 2 * high)
    other_core = (rep + 1 - 2 * core, fsdp)
    other_half = (rep + 2 - 4 * ((rep // 2) % 2), fsdp)
    near = j + 1 - 2 * (j % 2)
    far_mid = 2 - high
    far_outer = 3 - 3 * high
    arrival = (j, near, far_mid, far_outer)
    order = (far_outer, far_mid, near, j)

    def remote(src, dst, ssem, rsem, device):
        return pltpu.make_async_remote_copy(
            src_ref=src, dst_ref=dst, send_sem=ssem, recv_sem=rsem,
            device_id=device, device_id_type=MESH,
        )

    barrier = pltpu.get_barrier_semaphore()

    def greet(device):
        pl.semaphore_signal(barrier, inc=1, device_id=device, device_id_type=MESH)

    for d in range(1, NX):
        greet(along_x(d))
    greet(inward)

    @pl.when(mid)
    def _():
        greet(outward)

    greet(other_core)
    greet(other_half)

    @pl.when(z > 0)
    def _():
        greet(along_z(NZ - 1))

    @pl.when(z < NZ - 1)
    def _():
        greet(along_z(1))

    own_rows = pl.ds(pl.multiple_of(i * TOK, TOK), TOK)
    half_rows = lambda h: pl.ds(pl.multiple_of(h * TOK, TOK), TOK)
    slice_rows = lambda s: pl.ds(pl.multiple_of(s * SLICE, SLICE), SLICE)

    loads = [
        pltpu.make_async_copy(hidden, h_v, local_sem.at[0]),
        pltpu.make_async_copy(value_grad, vg_buf.at[own_rows], local_sem.at[1]),
        pltpu.make_async_copy(weight, w_buf.at[j], local_sem.at[2]),
        pltpu.make_async_copy(delta.at[half_rows(core)], d_own, local_sem.at[3]),
        pltpu.make_async_copy(momentum, mom_v, local_sem.at[4]),
    ]
    for load in loads:
        load.start()

    z_ends = (NZ - 1 - z) // (NZ - 1) + z // (NZ - 1)
    pl.semaphore_wait(barrier, 8 + is_mid - z_ends)

    vg_copies = [
        remote(value_grad, vg_buf.at[own_rows], x_send.at[d], x_recv.at[d], along_x(d))
        for d in range(1, NX)
    ]
    for copy in vg_copies:
        copy.start()
    def w_half(h):
        return pl.ds(h * (ROWS // 2), ROWS // 2)

    def w_own(h, way, device):
        return remote(
            weight.at[w_half(h)], w_buf.at[j, w_half(h)],
            w_ssem.at[way, h], w_rsem.at[j, h], device,
        )

    for h in range(2):
        w_own(h, 0, inward).start()

        @pl.when(mid)
        def _():
            w_own(h, 1, outward).start()

    core_half = remote(
        delta.at[half_rows(1 - core)], d_recv, c_ssem.at[0], c_rsem.at[0], other_core
    )
    core_half.start()

    loads[0].wait()

    def columns(f):
        return pl.ds(pl.multiple_of(f * ROWS, ROWS), ROWS)

    def add_square(f, total):
        block = h_v[:, columns(f)].astype(F32)
        return total + block * block

    squares = lax.fori_loop(0, 16, add_square, jnp.zeros((TOK, ROWS), F32))
    inv_v[...] = lax.rsqrt(jnp.sum(squares, axis=-1, keepdims=True) / D + EPSILON)

    @pl.loop(0, 16)
    def _(f):
        scaled = h_v[:, columns(f)].astype(F32) * inv_v[...]
        n_send[f] = (scaled * gain[:, columns(f)].astype(F32)).astype(BF16)

    n_copies = []
    for n, block in enumerate(order):
        for d in (1, 3, 2):
            copy = remote(
                n_send.at[((i + d) % NX) * NY + block], n_buf.at[block, own_rows],
                n_ssem.at[n, d], n_rsem.at[n, d], along_x(d),
            )
            copy.start()
            n_copies.append(copy)
    for block in range(NY):
        n_buf[block, own_rows] = n_send[i * NY + block]

    @pl.when(z > 0)
    def _():
        pl.semaphore_wait(below_sem, 1)

    @pl.when(z < NZ - 1)
    def _():
        pl.semaphore_signal(
            below_sem, inc=1, device_id=along_z(1), device_id_type=MESH
        )

    for d in range(2, NZ):
        @pl.when(z >= d)
        def _():
            pl.semaphore_signal(
                above_sem, inc=1, device_id=along_z(NZ - d), device_id_type=MESH
            )

    loads[3].wait()
    core_half.wait_recv()
    q_send[...] = (d_own[...].astype(F32) + d_recv[...].astype(F32)).astype(BF16)
    half_copy = remote(q_send, q_recv, c_ssem.at[1], c_rsem.at[1], other_half)
    half_copy.start()

    z_copies = [
        remote(
            p_send.at[slice_rows((z + d) % NZ)], z_recv.at[d - 1],
            z_ssem.at[d], z_rsem.at[d], along_z(d),
        )
        for d in range(1, NZ)
    ]

    late = z >= NZ // 2

    def send_slices():
        half_copy.wait_recv()
        p_send[...] = (q_send[...].astype(F32) + q_recv[...].astype(F32)).astype(BF16)

        @pl.when(z < NZ - 2)
        def _():
            pl.semaphore_wait(above_sem, NZ - 2 - z)

        for copy in z_copies:
            copy.start()

    a_copies = [
        remote(
            avg.at[core, slice_rows(z)], avg.at[core, slice_rows(z)],
            a_ssem.at[d], a_rsem.at[d], along_z(d),
        )
        for d in range(1, NZ)
    ]

    def send_average():
        for copy in z_copies:
            copy.wait_recv()
        total = q_send[slice_rows(z)].astype(F32) + q_recv[slice_rows(z)].astype(F32)
        for d in range(NZ - 1):
            total = total + z_recv[d].astype(F32)
        avg[core, slice_rows(z)] = total / 32.0
        for copy in a_copies:
            copy.start()

    core_full = remote(avg.at[core], avg.at[core], c_ssem.at[2], c_rsem.at[2], other_core)
    core_back = remote(
        avg.at[1 - core], avg.at[1 - core], c_ssem.at[2], c_rsem.at[2], other_core
    )

    def share_average():
        for copy in a_copies:
            copy.wait_recv()
        core_full.start()

    def w_forward(n, h):
        part = w_buf.at[arrival[n], w_half(h)]
        return remote(
            part, part, w_ssem.at[n + 1, h], w_rsem.at[arrival[n], h],
            inward if n == 1 else outward,
        )

    def forward_weight(n, h):
        @pl.when(mid)
        def _():
            w_forward(n, h).wait_recv()
            w_forward(n, h).start()

    def await_weight(n):
        @pl.when(outer)
        def _():
            for h in range(2):
                w_forward(n, h).wait_recv()

    g_copies = []

    def send_grad(n):
        block = arrival[n]
        ng_send[n] = lax.dot_general(
            vg_buf[...], w_buf[block], (((1,), (1,)), ((), ())), preferred_element_type=F32
        ).astype(BF16)
        for d in (1, 3, 2):
            copy = remote(
                ng_send.at[n, pl.ds(pl.multiple_of(((i + d) % NX) * TOK, TOK), TOK)],
                ng_buf.at[i * NY + block], g_ssem.at[n, d], g_rsem.at[n, d], along_x(d),
            )
            copy.start()
            g_copies.append(copy)
        ng_buf[i * NY + block] = ng_send[n, own_rows]

    def make_weight_grad(n):
        for d in range(1, NX):
            n_copies[3 * n + (0, 0, 2, 1)[d]].wait_recv()
        block = order[n]
        wg_acc[block] = lax.dot_general(
            n_buf[block], vg_buf[...], (((0,), (0,)), ((), ())), preferred_element_type=F32
        ) * (1.0 / TOK)

    def first_hop(n):
        return remote(
            wg_send.at[order[n]], wg_recv.at[n], r_ssem.at[n], r_rsem.at[n], inward
        )

    def start_chain(n):
        @pl.when(outer)
        def _():
            wg_send[order[n]] = wg_acc[order[n]].astype(BF16)
            first_hop(n).start()

    def next_hop(slot):
        block, target, device = (
            (far_outer, 3, inward), (far_mid, 4, inward), None, (near, 3, outward),
        )[slot]
        return block, remote(
            wg_send.at[block], wg_recv.at[target], r_ssem.at[slot], r_rsem.at[target], device
        )

    def r_arrive(slot):
        remote(
            wg_recv.at[slot], wg_recv.at[slot], r_ssem.at[0], r_rsem.at[slot], inward
        ).wait_recv()

    def pass_on(slot):
        @pl.when(mid)
        def _():
            block, copy = next_hop(slot)
            r_arrive(slot)
            wg_send[block] = (wg_acc[block] + wg_recv[slot].astype(F32)).astype(BF16)
            copy.start()

    for h in range(2):
        forward_weight(1, h)
        forward_weight(2, h)
    loads[1].wait()
    loads[2].wait()
    for copy in vg_copies:
        copy.wait_recv()
    send_grad(0)
    pl.when(late)(send_slices)
    forward_weight(3, 0)
    await_weight(1)
    send_grad(1)
    make_weight_grad(0)
    start_chain(0)
    pl.when(jnp.logical_not(late))(send_slices)
    forward_weight(3, 1)
    make_weight_grad(1)
    start_chain(1)
    pl.when(late)(send_average)
    await_weight(2)
    send_grad(2)
    make_weight_grad(2)
    start_chain(2)
    pass_on(0)
    make_weight_grad(3)
    pl.when(jnp.logical_not(late))(send_average)
    await_weight(3)
    send_grad(3)

    v_acc = jnp.dot(n_buf[0], w_buf[0], preferred_element_type=F32)
    for block in range(1, NY):
        v_acc = v_acc + jnp.dot(n_buf[block], w_buf[block], preferred_element_type=F32)
    v_send[...] = v_acc.astype(BF16)
    v_copies = []
    for d in (1, 3, 2):
        copy = remote(
            v_send.at[pl.ds(pl.multiple_of(((i + d) % NX) * TOK, TOK), TOK)],
            v_recv.at[d - 1], v_ssem.at[d], v_rsem.at[d], along_x(d),
        )
        copy.start()
        v_copies.append(copy)

    def gated_scaled(f):
        scaled = h_v[:, columns(f)].astype(F32) * inv_v[...]
        gated = ng_buf[f].astype(F32) * gain[:, columns(f)].astype(F32)
        return gated, scaled

    row_v[...] = jnp.zeros_like(row_v)

    def add_rows(f):
        gated, scaled = gated_scaled(f)
        row_v[...] += gated * scaled

    def take_grad(n):
        add_rows(i * NY + arrival[n])
        for d in range(1, NX):
            g_copies[3 * n + (0, 0, 2, 1)[d]].wait_recv()
            add_rows(((i + NX - d) % NX) * NY + arrival[n])

    take_grad(0)
    pass_on(1)
    pass_on(3)
    take_grad(1)
    share_average()
    take_grad(2)
    take_grad(3)
    mean = jnp.sum(row_v[...], axis=-1, keepdims=True) / D

    @pl.loop(0, 16)
    def _(f):
        gated, scaled = gated_scaled(f)
        hg_out[:, columns(f)] = (inv_v[...] * (gated - scaled * mean)).astype(BF16)

    @pl.when(outer)
    def _():
        r_arrive(3)
        wg_out[...] = (wg_acc[j] + wg_recv[3].astype(F32)).astype(BF16)

    @pl.when(mid)
    def _():
        r_arrive(2)
        r_arrive(4)
        wg_out[...] = (
            wg_acc[j] + wg_recv[2].astype(F32) + wg_recv[4].astype(F32)
        ).astype(BF16)

    core_back.wait_recv()
    loads[4].wait()
    for h in range(2):
        rows = pl.ds(h * TOK, TOK)
        new_momentum = MOMENT * mom_v[rows] + avg[h]
        nm_out[rows] = new_momentum
        os_out[rows] = -OUTER_RATE * (avg[h] + MOMENT * new_momentum)

    value_sum = v_send[own_rows].astype(F32)
    for copy in v_copies:
        copy.wait_recv()
    for d in range(NX - 1):
        value_sum = value_sum + v_recv[d].astype(F32)
    val_out[...] = value_sum.astype(BF16)

    for copy in (*vg_copies, w_own(0, 0, inward), w_own(1, 0, inward), core_half, *n_copies, *z_copies, *g_copies, *a_copies):
        copy.wait_send()
    for copy in (*v_copies, core_full, half_copy):
        copy.wait_send()

    @pl.when(mid)
    def _():
        for h in range(2):
            w_own(h, 1, outward).wait_send()
            for n in range(1, NY):
                w_forward(n, h).wait_send()
        for slot in (0, 1, 3):
            next_hop(slot)[1].wait_send()

    @pl.when(outer)
    def _():
        for n in range(3):
            first_hop(n).wait_send()


def store(*refs):
    sems = refs[-1]
    copies = [
        pltpu.make_async_copy(refs[k], refs[5 + k], sems.at[k]) for k in range(5)
    ]
    for copy in copies:
        copy.start()
    for copy in copies:
        copy.wait()


def per_device(hidden, gain, value_grad, value_weight, outer_delta, momentum):
    anywhere = pl.BlockSpec(memory_space=pl.ANY)
    vmem = pl.BlockSpec(memory_space=pltpu.VMEM)
    dma = pltpu.SemaphoreType.DMA
    shapes = (
        jax.ShapeDtypeStruct((TOK, D), BF16),
        jax.ShapeDtypeStruct((TOK, KV), BF16),
        jax.ShapeDtypeStruct((ROWS, KV), BF16),
        jax.ShapeDtypeStruct((ROWS, KV), F32),
        jax.ShapeDtypeStruct((ROWS, KV), F32),
    )
    outs = pl.pallas_call(
        exchange,
        out_shape=shapes,
        in_specs=[anywhere, vmem, anywhere, anywhere, anywhere, anywhere],
        out_specs=[vmem] * 5,
        scratch_shapes=[
            pltpu.VMEM((TOK, D), BF16),
            pltpu.VMEM((TOK, 1), F32),
            pltpu.VMEM((TOK, ROWS), F32),
            pltpu.VMEM((16, TOK, ROWS), BF16),
            pltpu.VMEM((NY, GROUP, ROWS), BF16),
            pltpu.VMEM((GROUP, KV), BF16),
            pltpu.VMEM((NY, ROWS, KV), BF16),
            pltpu.VMEM((NY, GROUP, ROWS), BF16),
            pltpu.VMEM((16, TOK, ROWS), BF16),
            pltpu.VMEM((GROUP, KV), BF16),
            pltpu.VMEM((NX - 1, TOK, KV), BF16),
            pltpu.VMEM((NY, ROWS, KV), F32),
            pltpu.VMEM((NY, ROWS, KV), BF16),
            pltpu.VMEM((5, ROWS, KV), BF16),
            pltpu.VMEM((TOK, KV), BF16),
            pltpu.VMEM((TOK, KV), BF16),
            pltpu.VMEM((TOK, KV), BF16),
            pltpu.VMEM((TOK, KV), BF16),
            pltpu.VMEM((TOK, KV), BF16),
            pltpu.VMEM((NZ - 1, SLICE, KV), BF16),
            pltpu.VMEM((2, TOK, KV), F32),
            pltpu.VMEM((ROWS, KV), F32),
            dma((5,)),
            dma((NX,)), dma((NX,)),
            dma((NY, NX)), dma((NY, NX)),
            dma((NY, NX)), dma((NY, NX)),
            dma((NX,)), dma((NX,)),
            dma((5, 2)), dma((NY, 2)),
            dma((5,)), dma((5,)),
            dma((3,)), dma((3,)),
            dma((NZ,)), dma((NZ,)),
            dma((NZ,)), dma((NZ,)),
            pltpu.SemaphoreType.REGULAR,
            pltpu.SemaphoreType.REGULAR,
        ],
        compiler_params=pltpu.CompilerParams(
            collective_id=0, has_side_effects=True, vmem_limit_bytes=40 * 1024 * 1024
        ),
    )(*[pltpu.with_memory_space_constraint(a, pltpu.HBM) for a in (hidden[0], gain, value_grad[0], value_weight[0], outer_delta[0], momentum)])
    hidden_grad, values, weight_grad, new_momentum, outer_step = pl.pallas_call(
        store,
        out_shape=shapes,
        in_specs=[anywhere] * 5,
        out_specs=[anywhere] * 5,
        scratch_shapes=[dma((5,))],
        compiler_params=pltpu.CompilerParams(vmem_limit_bytes=1024 * 1024),
    )(*outs)
    return (values[None], weight_grad[None], hidden_grad[None], new_momentum, outer_step)


def solution(mesh):
    in_specs = (
        P("rep", "fsdp", None),
        P("rep", None),
        P("rep", "fsdp", None),
        P("rep", "fsdp", None),
        P("rep", "fsdp", None),
        P("fsdp", None),
    )
    out_specs = (
        P("rep", "fsdp", None),
        P("rep", "fsdp", None),
        P("rep", "fsdp", None),
        P("fsdp", None),
        P("fsdp", None),
    )
    return jax.shard_map(
        per_device, mesh=mesh, in_specs=in_specs, out_specs=out_specs, check_vma=False
    )
```

```python
import jax
import jax.numpy as jnp
from jax import lax
from jax.experimental import pallas as pl
from jax.experimental.pallas import tpu as pltpu
from jax.sharding import PartitionSpec as P

EPSILON = 1e-05
MOMENT = 0.9
OUTER_RATE = 0.7

TOK = 128
D = 4096
KV = 512
ROWS = 256
NX = 4
NY = 4
NZ = 8
GROUP = NX * TOK
SLICE = 16

MESH = pl.DeviceIdType.MESH
F32 = jnp.float32
BF16 = jnp.bfloat16


def exchange(
    hidden, gain, value_grad, weight, delta, momentum,
    hg_out, val_out, wg_out, nm_out, os_out,
    h_v, inv_v, row_v, n_send, n_buf, vg_buf, w_buf, ng_send, ng_buf,
    v_part, v_send, v_mid, v_recv, wg_acc, wg_send, wg_recv,
    d_own, d_recv, q_send, q_recv, p_send, z_recv, avg, mom_v,
    local_sem, x_send, x_recv, n_ssem, n_rsem, g_ssem, g_rsem, v_ssem, v_rsem,
    w_ssem, w_rsem, r_ssem, r_rsem, c_ssem, c_rsem, z_ssem, z_rsem, a_ssem, a_rsem,
    below_sem, above_sem,
):
    rep = lax.axis_index("rep")
    fsdp = lax.axis_index("fsdp")
    i, j = fsdp // NY, fsdp % NY
    z, core = rep // 4, rep % 2
    high = j // 2
    mid = jnp.logical_or(j == 1, j == 2)
    outer = jnp.logical_not(mid)
    is_mid = high + j % 2 - 2 * high * (j % 2)

    def along_x(d):
        return (rep, ((i + d) % NX) * NY + j)

    def along_z(d):
        return (((z + d) % NZ) * 4 + rep % 4, fsdp)

    inward = (rep, i * NY + j + 1 - 2 * high)
    outward = (rep, i * NY + j - 1 + 2 * high)
    other_core = (rep + 1 - 2 * core, fsdp)
    other_half = (rep + 2 - 4 * ((rep // 2) % 2), fsdp)
    near = j + 1 - 2 * (j % 2)
    far_mid = 2 - high
    far_outer = 3 - 3 * high
    arrival = (j, near, far_mid, far_outer)
    order = (far_outer, far_mid, near, j)

    def remote(src, dst, ssem, rsem, device):
        return pltpu.make_async_remote_copy(
            src_ref=src, dst_ref=dst, send_sem=ssem, recv_sem=rsem,
            device_id=device, device_id_type=MESH,
        )

    barrier = pltpu.get_barrier_semaphore()

    def greet(device):
        pl.semaphore_signal(barrier, inc=1, device_id=device, device_id_type=MESH)

    for d in range(1, NX):
        greet(along_x(d))
    greet(inward)

    @pl.when(mid)
    def _():
        greet(outward)

    greet(other_core)
    late = z >= NZ // 2

    greet(other_half)
    for d in range(1, NZ):
        there = (z + d) % NZ
        both_late = jnp.logical_and(late, there >= NZ // 2)
        beside = jnp.logical_or(there == z + 1, there == z - 1)

        @pl.when(jnp.logical_or(both_late, beside))
        def _():
            greet(along_z(d))

    own_rows = pl.ds(pl.multiple_of(i * TOK, TOK), TOK)
    half_rows = lambda h: pl.ds(pl.multiple_of(h * TOK, TOK), TOK)
    slice_rows = lambda s: pl.ds(pl.multiple_of(s * SLICE, SLICE), SLICE)

    loads = [
        pltpu.make_async_copy(hidden, h_v, local_sem.at[0]),
        pltpu.make_async_copy(value_grad, vg_buf.at[own_rows], local_sem.at[1]),
        pltpu.make_async_copy(weight, w_buf.at[j], local_sem.at[2]),
        pltpu.make_async_copy(delta.at[half_rows(core)], d_own, local_sem.at[3]),
        pltpu.make_async_copy(momentum, mom_v, local_sem.at[4]),
    ]
    for load in loads:
        load.start()

    upper = z // 4
    first, fifth = 1 - (z + 7) // 8, upper * (1 - (z + 3) // 8)
    z_greeted = (1 - upper) * (2 - first) + upper * (3 + fifth)
    pl.semaphore_wait(barrier, 6 + is_mid + z_greeted)

    vg_first = [
        remote(value_grad, vg_buf.at[own_rows], x_send.at[d], x_recv.at[d], along_x(d))
        for d in (1, 3)
    ]
    for copy in vg_first:
        copy.start()
    half_tok = TOK // 2

    def part_rows(d, h):
        return pl.ds(pl.multiple_of(((i + d) % NX) * TOK + h * half_tok, half_tok), half_tok)

    vg_second = [
        remote(
            vg_buf.at[part_rows(NX - d, h)], vg_buf.at[part_rows(NX - d, h)],
            x_send.at[2 * h], x_recv.at[2 * h], along_x(d),
        )
        for d, h in ((1, 0), (3, 1))
    ]
    def w_half(h):
        return pl.ds(h * (ROWS // 2), ROWS // 2)

    def w_own(h, way, device):
        return remote(
            weight.at[w_half(h)], w_buf.at[j, w_half(h)],
            w_ssem.at[way, h], w_rsem.at[j, h], device,
        )

    for h in range(2):
        w_own(h, 0, inward).start()

        @pl.when(mid)
        def _():
            w_own(h, 1, outward).start()

    core_half = remote(
        delta.at[half_rows(1 - core)], d_recv, c_ssem.at[0], c_rsem.at[0], other_core
    )
    core_half.start()

    def tell(semaphore, device):
        pl.semaphore_signal(semaphore, inc=1, device_id=device, device_id_type=MESH)

    @pl.when(jnp.logical_and(z > 0, z <= 4))
    def _():
        pl.semaphore_wait(below_sem, 1)

    @pl.when(z < 4)
    def _():
        tell(below_sem, along_z(1))

    @pl.when(z == 4)
    def _():
        for d in range(1, 4):
            tell(below_sem, along_z(d))

    loads[0].wait()

    def columns(f):
        return pl.ds(pl.multiple_of(f * ROWS, ROWS), ROWS)

    def add_square(f, total):
        block = h_v[:, columns(f)].astype(F32)
        return total + block * block

    squares = lax.fori_loop(0, 16, add_square, jnp.zeros((TOK, ROWS), F32))
    inv_v[...] = lax.rsqrt(jnp.sum(squares, axis=-1, keepdims=True) / D + EPSILON)

    @pl.loop(0, 16)
    def _(f):
        scaled = h_v[:, columns(f)].astype(F32) * inv_v[...]
        n_send[f] = (scaled * gain[:, columns(f)].astype(F32)).astype(BF16)

    @pl.when(z > 4)
    def _():
        pl.semaphore_wait(below_sem, 1)

    for d in range(2, NZ):
        @pl.when(jnp.logical_and(z >= d, z < d + 4))
        def _():
            tell(above_sem, along_z(NZ - d))

    n_copies = []
    for n, block in enumerate(order):
        for d in (1, 3, 2):
            copy = remote(
                n_send.at[((i + d) % NX) * NY + block], n_buf.at[block, own_rows],
                n_ssem.at[n, d], n_rsem.at[n, d], along_x(d),
            )
            copy.start()
            n_copies.append(copy)
        if n == 0:
            for first, second in zip(vg_first, vg_second):
                first.wait_recv()
                second.start()
    for block in range(NY):
        n_buf[block, own_rows] = n_send[i * NY + block]

    loads[3].wait()
    core_half.wait_recv()
    q_send[...] = (d_own[...].astype(F32) + d_recv[...].astype(F32)).astype(BF16)
    half_copy = remote(q_send, q_recv, c_ssem.at[1], c_rsem.at[1], other_half)
    half_copy.start()

    z_copies = [
        remote(
            p_send.at[slice_rows((z + d) % NZ)], z_recv.at[d - 1],
            z_ssem.at[d], z_rsem.at[d], along_z(d),
        )
        for d in range(1, NZ)
    ]

    def send_slices():
        half_copy.wait_recv()
        p_send[...] = (q_send[...].astype(F32) + q_recv[...].astype(F32)).astype(BF16)

        @pl.when(z < 4)
        def _():
            pl.semaphore_wait(above_sem, 6 - z)

        for copy in z_copies:
            copy.start()

    a_copies = [
        remote(
            avg.at[core, slice_rows(z)], avg.at[core, slice_rows(z)],
            a_ssem.at[d], a_rsem.at[d], along_z(d),
        )
        for d in range(1, NZ)
    ]

    def send_average():
        for copy in z_copies:
            copy.wait_recv()
        total = q_send[slice_rows(z)].astype(F32) + q_recv[slice_rows(z)].astype(F32)
        for d in range(NZ - 1):
            total = total + z_recv[d].astype(F32)
        avg[core, slice_rows(z)] = (total / 32.0).astype(BF16)
        for copy in a_copies:
            copy.start()

    core_full = remote(avg.at[core], avg.at[core], c_ssem.at[2], c_rsem.at[2], other_core)
    core_back = remote(
        avg.at[1 - core], avg.at[1 - core], c_ssem.at[2], c_rsem.at[2], other_core
    )

    def share_average():
        for copy in a_copies:
            copy.wait_recv()
        core_full.start()

    def w_forward(n, h):
        part = w_buf.at[arrival[n], w_half(h)]
        return remote(
            part, part, w_ssem.at[n + 1, h], w_rsem.at[arrival[n], h],
            inward if n == 1 else outward,
        )

    def forward_weight(n, h):
        @pl.when(mid)
        def _():
            w_forward(n, h).wait_recv()
            w_forward(n, h).start()

    def await_weight(n):
        @pl.when(outer)
        def _():
            for h in range(2):
                w_forward(n, h).wait_recv()

    g_copies = []

    def send_grad(n):
        block = arrival[n]
        ng_send[n] = lax.dot_general(
            vg_buf[...], w_buf[block], (((1,), (1,)), ((), ())), preferred_element_type=F32
        ).astype(BF16)
        for d in (1, 3, 2):
            copy = remote(
                ng_send.at[n, pl.ds(pl.multiple_of(((i + d) % NX) * TOK, TOK), TOK)],
                ng_buf.at[i * NY + block], g_ssem.at[n, d], g_rsem.at[n, d], along_x(d),
            )
            copy.start()
            g_copies.append(copy)
        ng_buf[i * NY + block] = ng_send[n, own_rows]

    def make_weight_grad(n):
        for d in range(1, NX):
            n_copies[3 * n + (0, 0, 2, 1)[d]].wait_recv()
        block = order[n]
        wg_acc[block] = lax.dot_general(
            n_buf[block], vg_buf[...], (((0,), (0,)), ((), ())), preferred_element_type=F32
        ) * (1.0 / TOK)

    def first_hop(n):
        return remote(
            wg_send.at[order[n]], wg_recv.at[n], r_ssem.at[n], r_rsem.at[n], inward
        )

    def start_chain(n):
        @pl.when(outer)
        def _():
            wg_send[order[n]] = wg_acc[order[n]].astype(BF16)
            first_hop(n).start()

    def next_hop(slot):
        block, target, device = (
            (far_outer, 3, inward), (far_mid, 4, inward), None, (near, 3, outward),
        )[slot]
        return block, remote(
            wg_send.at[block], wg_recv.at[target], r_ssem.at[slot], r_rsem.at[target], device
        )

    def r_arrive(slot):
        remote(
            wg_recv.at[slot], wg_recv.at[slot], r_ssem.at[0], r_rsem.at[slot], inward
        ).wait_recv()

    def pass_on(slot):
        @pl.when(mid)
        def _():
            block, copy = next_hop(slot)
            r_arrive(slot)
            wg_send[block] = (wg_acc[block] + wg_recv[slot].astype(F32)).astype(BF16)
            copy.start()

    for h in range(2):
        forward_weight(1, h)
        forward_weight(2, h)
    loads[1].wait()
    loads[2].wait()
    for copy in vg_second:
        copy.wait_recv()
    send_grad(0)
    forward_weight(3, 0)
    await_weight(1)
    make_weight_grad(0)
    start_chain(0)
    send_grad(1)
    pl.when(late)(send_slices)
    forward_weight(3, 1)
    make_weight_grad(1)
    start_chain(1)
    pl.when(jnp.logical_not(late))(send_slices)
    await_weight(2)
    send_grad(2)
    make_weight_grad(2)
    start_chain(2)
    pass_on(0)
    pl.when(late)(send_average)
    make_weight_grad(3)
    await_weight(3)

    v_acc = jnp.dot(n_buf[0], w_buf[0], preferred_element_type=F32)
    for block in range(1, NY):
        v_acc = v_acc + jnp.dot(n_buf[block], w_buf[block], preferred_element_type=F32)
    v_part[...] = v_acc
    v_copies = []
    for d, h in ((1, 0), (3, 1)):
        rows = part_rows(2, h)
        v_send[rows] = v_part[rows].astype(BF16)
        copy = remote(v_send.at[rows], v_mid.at[h], v_ssem.at[h], v_rsem.at[h], along_x(d))
        copy.start()
        v_copies.append(copy)
    send_grad(3)
    pl.when(jnp.logical_not(late))(send_average)

    def send_values():
        for d, h in ((1, 0), (3, 1)):
            v_copies[h].wait_recv()
            added, kept = part_rows(d, h), part_rows(d, 1 - h)
            v_send[added] = (v_part[added] + v_mid[h].astype(F32)).astype(BF16)
            v_send[kept] = v_part[kept].astype(BF16)
            rows = pl.ds(pl.multiple_of(((i + d) % NX) * TOK, TOK), TOK)
            copy = remote(
                v_send.at[rows], v_recv.at[h], v_ssem.at[2 + h], v_rsem.at[2 + h], along_x(d)
            )
            copy.start()
            v_copies.append(copy)

    def gated_scaled(f):
        scaled = h_v[:, columns(f)].astype(F32) * inv_v[...]
        gated = ng_buf[f].astype(F32) * gain[:, columns(f)].astype(F32)
        return gated, scaled

    row_v[...] = jnp.zeros_like(row_v)

    def add_rows(f):
        gated, scaled = gated_scaled(f)
        row_v[...] += gated * scaled

    def take_grad(n):
        add_rows(i * NY + arrival[n])
        for d in range(1, NX):
            g_copies[3 * n + (0, 0, 2, 1)[d]].wait_recv()
            add_rows(((i + NX - d) % NX) * NY + arrival[n])

    pass_on(1)
    pass_on(3)
    take_grad(0)
    take_grad(1)
    take_grad(2)
    send_values()
    share_average()
    take_grad(3)
    mean = jnp.sum(row_v[...], axis=-1, keepdims=True) / D

    @pl.loop(0, 16)
    def _(f):
        gated, scaled = gated_scaled(f)
        hg_out[:, columns(f)] = (inv_v[...] * (gated - scaled * mean)).astype(BF16)

    @pl.when(outer)
    def _():
        r_arrive(3)
        wg_out[...] = (wg_acc[j] + wg_recv[3].astype(F32)).astype(BF16)

    @pl.when(mid)
    def _():
        r_arrive(2)
        r_arrive(4)
        wg_out[...] = (
            wg_acc[j] + wg_recv[2].astype(F32) + wg_recv[4].astype(F32)
        ).astype(BF16)

    core_back.wait_recv()
    loads[4].wait()
    for h in range(2):
        rows = pl.ds(h * TOK, TOK)
        average = avg[h].astype(F32)
        new_momentum = MOMENT * mom_v[rows] + average
        nm_out[rows] = new_momentum
        os_out[rows] = -OUTER_RATE * (average + MOMENT * new_momentum)

    value_sum = v_part[own_rows]
    for h in range(2):
        v_copies[2 + h].wait_recv()
        value_sum = value_sum + v_recv[h].astype(F32)
    val_out[...] = value_sum.astype(BF16)

    for copy in (*vg_first, *vg_second, w_own(0, 0, inward), w_own(1, 0, inward), core_half, *n_copies, *z_copies, *g_copies, *a_copies):
        copy.wait_send()
    for copy in (*v_copies, core_full, half_copy):
        copy.wait_send()

    @pl.when(mid)
    def _():
        for h in range(2):
            w_own(h, 1, outward).wait_send()
            for n in range(1, NY):
                w_forward(n, h).wait_send()
        for slot in (0, 1, 3):
            next_hop(slot)[1].wait_send()

    @pl.when(outer)
    def _():
        for n in range(3):
            first_hop(n).wait_send()


def store(*refs):
    sems = refs[-1]
    copies = [
        pltpu.make_async_copy(refs[k], refs[5 + k], sems.at[k]) for k in range(5)
    ]
    for copy in copies:
        copy.start()
    for copy in copies:
        copy.wait()


def per_device(hidden, gain, value_grad, value_weight, outer_delta, momentum):
    anywhere = pl.BlockSpec(memory_space=pl.ANY)
    vmem = pl.BlockSpec(memory_space=pltpu.VMEM)
    dma = pltpu.SemaphoreType.DMA
    shapes = (
        jax.ShapeDtypeStruct((TOK, D), BF16),
        jax.ShapeDtypeStruct((TOK, KV), BF16),
        jax.ShapeDtypeStruct((ROWS, KV), BF16),
        jax.ShapeDtypeStruct((ROWS, KV), F32),
        jax.ShapeDtypeStruct((ROWS, KV), F32),
    )
    outs = pl.pallas_call(
        exchange,
        out_shape=shapes,
        in_specs=[anywhere, vmem, anywhere, anywhere, anywhere, anywhere],
        out_specs=[vmem] * 5,
        scratch_shapes=[
            pltpu.VMEM((TOK, D), BF16),
            pltpu.VMEM((TOK, 1), F32),
            pltpu.VMEM((TOK, ROWS), F32),
            pltpu.VMEM((16, TOK, ROWS), BF16),
            pltpu.VMEM((NY, GROUP, ROWS), BF16),
            pltpu.VMEM((GROUP, KV), BF16),
            pltpu.VMEM((NY, ROWS, KV), BF16),
            pltpu.VMEM((NY, GROUP, ROWS), BF16),
            pltpu.VMEM((16, TOK, ROWS), BF16),
            pltpu.VMEM((GROUP, KV), F32),
            pltpu.VMEM((GROUP, KV), BF16),
            pltpu.VMEM((2, TOK // 2, KV), BF16),
            pltpu.VMEM((2, TOK, KV), BF16),
            pltpu.VMEM((NY, ROWS, KV), F32),
            pltpu.VMEM((NY, ROWS, KV), BF16),
            pltpu.VMEM((5, ROWS, KV), BF16),
            pltpu.VMEM((TOK, KV), BF16),
            pltpu.VMEM((TOK, KV), BF16),
            pltpu.VMEM((TOK, KV), BF16),
            pltpu.VMEM((TOK, KV), BF16),
            pltpu.VMEM((TOK, KV), BF16),
            pltpu.VMEM((NZ - 1, SLICE, KV), BF16),
            pltpu.VMEM((2, TOK, KV), BF16),
            pltpu.VMEM((ROWS, KV), F32),
            dma((5,)),
            dma((NX,)), dma((NX,)),
            dma((NY, NX)), dma((NY, NX)),
            dma((NY, NX)), dma((NY, NX)),
            dma((NX,)), dma((NX,)),
            dma((5, 2)), dma((NY, 2)),
            dma((5,)), dma((5,)),
            dma((3,)), dma((3,)),
            dma((NZ,)), dma((NZ,)),
            dma((NZ,)), dma((NZ,)),
            pltpu.SemaphoreType.REGULAR,
            pltpu.SemaphoreType.REGULAR,
        ],
        compiler_params=pltpu.CompilerParams(
            collective_id=0, has_side_effects=True, vmem_limit_bytes=40 * 1024 * 1024
        ),
    )(*[pltpu.with_memory_space_constraint(a, pltpu.HBM) for a in (hidden[0], gain, value_grad[0], value_weight[0], outer_delta[0], momentum)])
    hidden_grad, values, weight_grad, new_momentum, outer_step = pl.pallas_call(
        store,
        out_shape=shapes,
        in_specs=[anywhere] * 5,
        out_specs=[anywhere] * 5,
        scratch_shapes=[dma((5,))],
        compiler_params=pltpu.CompilerParams(vmem_limit_bytes=1024 * 1024),
    )(*outs)
    return (values[None], weight_grad[None], hidden_grad[None], new_momentum, outer_step)


def solution(mesh):
    in_specs = (
        P("rep", "fsdp", None),
        P("rep", None),
        P("rep", "fsdp", None),
        P("rep", "fsdp", None),
        P("rep", "fsdp", None),
        P("fsdp", None),
    )
    out_specs = (
        P("rep", "fsdp", None),
        P("rep", "fsdp", None),
        P("rep", "fsdp", None),
        P("fsdp", None),
        P("fsdp", None),
    )
    return jax.shard_map(
        per_device, mesh=mesh, in_specs=in_specs, out_specs=out_specs, check_vma=False
    )
```

```python
import jax
import jax.numpy as jnp
from jax import lax
from jax.experimental import pallas as pl
from jax.experimental.pallas import tpu as pltpu
from jax.sharding import PartitionSpec as P

EPSILON = 1e-05
MOMENT = 0.9
OUTER_RATE = 0.7

TOK = 128
D = 4096
KV = 512
ROWS = 256
NX = 4
NY = 4
NZ = 8
GROUP = NX * TOK
SLICE = 16

MESH = pl.DeviceIdType.MESH
F32 = jnp.float32
BF16 = jnp.bfloat16


def exchange(
    hidden, gain, value_grad, weight, delta, momentum,
    hg_out, val_out, wg_out, nm_out, os_out,
    h_v, inv_v, row_v, n_send, n_buf, vg_buf, w_buf, ng_send, ng_buf,
    v_part, v_send, v_mid, v_recv, wg_acc, wg_send, wg_recv,
    d_own, d_recv, q_send, q_recv, p_send, z_recv, avg, mom_v,
    local_sem, x_send, x_recv, n_ssem, n_rsem, g_ssem, g_rsem, v_ssem, v_rsem,
    w_ssem, w_rsem, r_ssem, r_rsem, c_ssem, c_rsem, z_ssem, z_rsem, a_ssem, a_rsem,
    below_sem, above_sem,
):
    rep = lax.axis_index("rep")
    fsdp = lax.axis_index("fsdp")
    i, j = fsdp // NY, fsdp % NY
    z, core = rep // 4, rep % 2
    high = j // 2
    mid = jnp.logical_or(j == 1, j == 2)
    outer = jnp.logical_not(mid)
    is_mid = high + j % 2 - 2 * high * (j % 2)

    def along_x(d):
        return (rep, ((i + d) % NX) * NY + j)

    def along_z(d):
        return (((z + d) % NZ) * 4 + rep % 4, fsdp)

    inward = (rep, i * NY + j + 1 - 2 * high)
    outward = (rep, i * NY + j - 1 + 2 * high)
    other_core = (rep + 1 - 2 * core, fsdp)
    other_half = (rep + 2 - 4 * ((rep // 2) % 2), fsdp)
    near = j + 1 - 2 * (j % 2)
    far_mid = 2 - high
    far_outer = 3 - 3 * high
    arrival = (j, near, far_mid, far_outer)
    order = (far_outer, far_mid, near, j)

    def remote(src, dst, ssem, rsem, device):
        return pltpu.make_async_remote_copy(
            src_ref=src, dst_ref=dst, send_sem=ssem, recv_sem=rsem,
            device_id=device, device_id_type=MESH,
        )

    barrier = pltpu.get_barrier_semaphore()

    def greet(device):
        pl.semaphore_signal(barrier, inc=1, device_id=device, device_id_type=MESH)

    for d in range(1, NX):
        greet(along_x(d))
    greet(inward)

    @pl.when(mid)
    def _():
        greet(outward)

    greet(other_core)
    late = z >= NZ // 2

    greet(other_half)
    for d in range(1, NZ):
        there = (z + d) % NZ
        both_late = jnp.logical_and(late, there >= NZ // 2)
        beside = jnp.logical_or(there == z + 1, there == z - 1)

        @pl.when(jnp.logical_or(both_late, beside))
        def _():
            greet(along_z(d))

    own_rows = pl.ds(pl.multiple_of(i * TOK, TOK), TOK)
    half_rows = lambda h: pl.ds(pl.multiple_of(h * TOK, TOK), TOK)
    slice_rows = lambda s: pl.ds(pl.multiple_of(s * SLICE, SLICE), SLICE)

    loads = [
        pltpu.make_async_copy(hidden, h_v, local_sem.at[0]),
        pltpu.make_async_copy(value_grad, vg_buf.at[own_rows], local_sem.at[1]),
        pltpu.make_async_copy(weight, w_buf.at[j], local_sem.at[2]),
        pltpu.make_async_copy(delta.at[half_rows(core)], d_own, local_sem.at[3]),
        pltpu.make_async_copy(momentum, mom_v, local_sem.at[4]),
    ]
    for load in loads:
        load.start()

    upper = z // 4
    first, fifth = 1 - (z + 7) // 8, upper * (1 - (z + 3) // 8)
    z_greeted = (1 - upper) * (2 - first) + upper * (3 + fifth)
    pl.semaphore_wait(barrier, 6 + is_mid + z_greeted)

    vg_first = [
        remote(value_grad, vg_buf.at[own_rows], x_send.at[d], x_recv.at[d], along_x(d))
        for d in (1, 3)
    ]
    for copy in vg_first:
        copy.start()
    half_tok = TOK // 2

    def part_rows(d, h):
        return pl.ds(pl.multiple_of(((i + d) % NX) * TOK + h * half_tok, half_tok), half_tok)

    vg_second = [
        remote(
            vg_buf.at[part_rows(NX - d, h)], vg_buf.at[part_rows(NX - d, h)],
            x_send.at[2 * h], x_recv.at[2 * h], along_x(d),
        )
        for d, h in ((1, 0), (3, 1))
    ]
    def w_half(h):
        return pl.ds(h * (ROWS // 2), ROWS // 2)

    def w_own(h, way, device):
        return remote(
            weight.at[w_half(h)], w_buf.at[j, w_half(h)],
            w_ssem.at[way, h], w_rsem.at[j, h], device,
        )

    for h in range(2):
        w_own(h, 0, inward).start()

        @pl.when(mid)
        def _():
            w_own(h, 1, outward).start()

    core_half = remote(
        delta.at[half_rows(1 - core)], d_recv, c_ssem.at[0], c_rsem.at[0], other_core
    )
    core_half.start()

    def tell(semaphore, device):
        pl.semaphore_signal(semaphore, inc=1, device_id=device, device_id_type=MESH)

    @pl.when(jnp.logical_and(z > 0, z <= 4))
    def _():
        pl.semaphore_wait(below_sem, 1)

    @pl.when(z < 4)
    def _():
        tell(below_sem, along_z(1))

    @pl.when(z == 4)
    def _():
        for d in range(1, 4):
            tell(below_sem, along_z(d))

    loads[0].wait()

    def columns(f):
        return pl.ds(pl.multiple_of(f * ROWS, ROWS), ROWS)

    def add_square(f, total):
        block = h_v[:, columns(f)].astype(F32)
        return total + block * block

    squares = lax.fori_loop(0, 16, add_square, jnp.zeros((TOK, ROWS), F32))
    inv_v[...] = lax.rsqrt(jnp.sum(squares, axis=-1, keepdims=True) / D + EPSILON)

    def make_normed(block):
        @pl.loop(0, NX)
        def _(part):
            f = part * NY + block
            scaled = h_v[:, columns(f)].astype(F32) * inv_v[...]
            n_send[f] = (scaled * gain[:, columns(f)].astype(F32)).astype(BF16)

    @pl.when(z > 4)
    def _():
        pl.semaphore_wait(below_sem, 1)

    for d in range(2, NZ):
        @pl.when(jnp.logical_and(z >= d, z < d + 4))
        def _():
            tell(above_sem, along_z(NZ - d))

    loads[3].wait()
    core_half.wait_recv()
    q_send[...] = (d_own[...].astype(F32) + d_recv[...].astype(F32)).astype(BF16)
    half_copy = remote(q_send, q_recv, c_ssem.at[1], c_rsem.at[1], other_half)
    half_copy.start()

    n_copies = []
    for n, block in enumerate(order):
        make_normed(block)
        for d in (1, 3, 2):
            copy = remote(
                n_send.at[((i + d) % NX) * NY + block], n_buf.at[block, own_rows],
                n_ssem.at[n, d], n_rsem.at[n, d], along_x(d),
            )
            copy.start()
            n_copies.append(copy)
        if n == 0:
            for first, second in zip(vg_first, vg_second):
                first.wait_recv()
                second.start()
    for block in range(NY):
        n_buf[block, own_rows] = n_send[i * NY + block]

    z_copies = [
        remote(
            p_send.at[slice_rows((z + d) % NZ)], z_recv.at[d - 1],
            z_ssem.at[d], z_rsem.at[d], along_z(d),
        )
        for d in range(1, NZ)
    ]

    def send_slices():
        half_copy.wait_recv()
        p_send[...] = (q_send[...].astype(F32) + q_recv[...].astype(F32)).astype(BF16)

        @pl.when(z < 4)
        def _():
            pl.semaphore_wait(above_sem, 6 - z)

        for copy in z_copies:
            copy.start()

    a_copies = [
        remote(
            avg.at[core, slice_rows(z)], avg.at[core, slice_rows(z)],
            a_ssem.at[d], a_rsem.at[d], along_z(d),
        )
        for d in range(1, NZ)
    ]

    def send_average():
        for copy in z_copies:
            copy.wait_recv()
        total = q_send[slice_rows(z)].astype(F32) + q_recv[slice_rows(z)].astype(F32)
        for d in range(NZ - 1):
            total = total + z_recv[d].astype(F32)
        avg[core, slice_rows(z)] = (total / 32.0).astype(BF16)
        for copy in a_copies:
            copy.start()

    core_full = remote(avg.at[core], avg.at[core], c_ssem.at[2], c_rsem.at[2], other_core)
    core_back = remote(
        avg.at[1 - core], avg.at[1 - core], c_ssem.at[2], c_rsem.at[2], other_core
    )

    def share_average():
        for copy in a_copies:
            copy.wait_recv()
        core_full.start()

    def w_forward(n, h):
        part = w_buf.at[arrival[n], w_half(h)]
        return remote(
            part, part, w_ssem.at[n + 1, h], w_rsem.at[arrival[n], h],
            inward if n == 1 else outward,
        )

    def forward_weight(n, h):
        @pl.when(mid)
        def _():
            w_forward(n, h).wait_recv()
            w_forward(n, h).start()

    def await_weight(n):
        @pl.when(outer)
        def _():
            for h in range(2):
                w_forward(n, h).wait_recv()

    g_copies = []

    def send_grad(n):
        block = arrival[n]
        ng_send[n] = lax.dot_general(
            vg_buf[...], w_buf[block], (((1,), (1,)), ((), ())), preferred_element_type=F32
        ).astype(BF16)
        for d in (1, 3, 2):
            copy = remote(
                ng_send.at[n, pl.ds(pl.multiple_of(((i + d) % NX) * TOK, TOK), TOK)],
                ng_buf.at[i * NY + block], g_ssem.at[n, d], g_rsem.at[n, d], along_x(d),
            )
            copy.start()
            g_copies.append(copy)
        ng_buf[i * NY + block] = ng_send[n, own_rows]

    def make_weight_grad(n):
        for d in range(1, NX):
            n_copies[3 * n + (0, 0, 2, 1)[d]].wait_recv()
        block = order[n]
        wg_acc[block] = lax.dot_general(
            n_buf[block], vg_buf[...], (((0,), (0,)), ((), ())), preferred_element_type=F32
        ) * (1.0 / TOK)

    def first_hop(n):
        return remote(
            wg_send.at[order[n]], wg_recv.at[n], r_ssem.at[n], r_rsem.at[n], inward
        )

    def start_chain(n):
        @pl.when(outer)
        def _():
            wg_send[order[n]] = wg_acc[order[n]].astype(BF16)
            first_hop(n).start()

    def next_hop(slot):
        block, target, device = (
            (far_outer, 3, inward), (far_mid, 4, inward), None, (near, 3, outward),
        )[slot]
        return block, remote(
            wg_send.at[block], wg_recv.at[target], r_ssem.at[slot], r_rsem.at[target], device
        )

    def r_arrive(slot):
        remote(
            wg_recv.at[slot], wg_recv.at[slot], r_ssem.at[0], r_rsem.at[slot], inward
        ).wait_recv()

    def pass_on(slot):
        @pl.when(mid)
        def _():
            block, copy = next_hop(slot)
            r_arrive(slot)
            wg_send[block] = (wg_acc[block] + wg_recv[slot].astype(F32)).astype(BF16)
            copy.start()

    for h in range(2):
        forward_weight(1, h)
        forward_weight(2, h)
    loads[1].wait()
    loads[2].wait()
    for copy in vg_second:
        copy.wait_recv()
    send_grad(0)
    forward_weight(3, 0)
    await_weight(1)
    make_weight_grad(0)
    start_chain(0)
    pl.when(late)(send_slices)
    send_grad(1)
    forward_weight(3, 1)
    make_weight_grad(1)
    start_chain(1)
    pl.when(jnp.logical_not(late))(send_slices)
    await_weight(2)
    send_grad(2)
    make_weight_grad(2)
    start_chain(2)
    pass_on(0)
    pl.when(late)(send_average)
    make_weight_grad(3)
    await_weight(3)

    v_acc = jnp.dot(n_buf[0], w_buf[0], preferred_element_type=F32)
    for block in range(1, NY):
        v_acc = v_acc + jnp.dot(n_buf[block], w_buf[block], preferred_element_type=F32)
    v_part[...] = v_acc
    v_copies = []
    for d, h in ((1, 0), (3, 1)):
        rows = part_rows(2, h)
        v_send[rows] = v_part[rows].astype(BF16)
        copy = remote(v_send.at[rows], v_mid.at[h], v_ssem.at[h], v_rsem.at[h], along_x(d))
        copy.start()
        v_copies.append(copy)
    send_grad(3)
    pl.when(jnp.logical_not(late))(send_average)

    def send_values():
        for d, h in ((1, 0), (3, 1)):
            v_copies[h].wait_recv()
            added, kept = part_rows(d, h), part_rows(d, 1 - h)
            v_send[added] = (v_part[added] + v_mid[h].astype(F32)).astype(BF16)
            v_send[kept] = v_part[kept].astype(BF16)
            rows = pl.ds(pl.multiple_of(((i + d) % NX) * TOK, TOK), TOK)
            copy = remote(
                v_send.at[rows], v_recv.at[h], v_ssem.at[2 + h], v_rsem.at[2 + h], along_x(d)
            )
            copy.start()
            v_copies.append(copy)

    def gated_scaled(f):
        scaled = h_v[:, columns(f)].astype(F32) * inv_v[...]
        gated = ng_buf[f].astype(F32) * gain[:, columns(f)].astype(F32)
        return gated, scaled

    row_v[...] = jnp.zeros_like(row_v)

    def add_rows(f):
        gated, scaled = gated_scaled(f)
        row_v[...] += gated * scaled

    def take_grad(n):
        add_rows(i * NY + arrival[n])
        for d in range(1, NX):
            g_copies[3 * n + (0, 0, 2, 1)[d]].wait_recv()
            add_rows(((i + NX - d) % NX) * NY + arrival[n])

    pass_on(1)
    pass_on(3)
    take_grad(0)
    take_grad(1)
    take_grad(2)
    send_values()
    share_average()
    take_grad(3)
    mean = jnp.sum(row_v[...], axis=-1, keepdims=True) / D

    @pl.loop(0, 16)
    def _(f):
        gated, scaled = gated_scaled(f)
        hg_out[:, columns(f)] = (inv_v[...] * (gated - scaled * mean)).astype(BF16)

    @pl.when(outer)
    def _():
        r_arrive(3)
        wg_out[...] = (wg_acc[j] + wg_recv[3].astype(F32)).astype(BF16)

    @pl.when(mid)
    def _():
        r_arrive(2)
        r_arrive(4)
        wg_out[...] = (
            wg_acc[j] + wg_recv[2].astype(F32) + wg_recv[4].astype(F32)
        ).astype(BF16)

    core_back.wait_recv()
    loads[4].wait()
    for h in range(2):
        rows = pl.ds(h * TOK, TOK)
        average = avg[h].astype(F32)
        new_momentum = MOMENT * mom_v[rows] + average
        nm_out[rows] = new_momentum
        os_out[rows] = -OUTER_RATE * (average + MOMENT * new_momentum)

    value_sum = v_part[own_rows]
    for h in range(2):
        v_copies[2 + h].wait_recv()
        value_sum = value_sum + v_recv[h].astype(F32)
    val_out[...] = value_sum.astype(BF16)

    for copy in (*vg_first, *vg_second, w_own(0, 0, inward), w_own(1, 0, inward), core_half, *n_copies, *z_copies, *g_copies, *a_copies):
        copy.wait_send()
    for copy in (*v_copies, core_full, half_copy):
        copy.wait_send()

    @pl.when(mid)
    def _():
        for h in range(2):
            w_own(h, 1, outward).wait_send()
            for n in range(1, NY):
                w_forward(n, h).wait_send()
        for slot in (0, 1, 3):
            next_hop(slot)[1].wait_send()

    @pl.when(outer)
    def _():
        for n in range(3):
            first_hop(n).wait_send()


def store(*refs):
    sems = refs[-1]
    copies = [
        pltpu.make_async_copy(refs[k], refs[5 + k], sems.at[k]) for k in range(5)
    ]
    for copy in copies:
        copy.start()
    for copy in copies:
        copy.wait()


def per_device(hidden, gain, value_grad, value_weight, outer_delta, momentum):
    anywhere = pl.BlockSpec(memory_space=pl.ANY)
    vmem = pl.BlockSpec(memory_space=pltpu.VMEM)
    dma = pltpu.SemaphoreType.DMA
    shapes = (
        jax.ShapeDtypeStruct((TOK, D), BF16),
        jax.ShapeDtypeStruct((TOK, KV), BF16),
        jax.ShapeDtypeStruct((ROWS, KV), BF16),
        jax.ShapeDtypeStruct((ROWS, KV), F32),
        jax.ShapeDtypeStruct((ROWS, KV), F32),
    )
    outs = pl.pallas_call(
        exchange,
        out_shape=shapes,
        in_specs=[anywhere, vmem, anywhere, anywhere, anywhere, anywhere],
        out_specs=[vmem] * 5,
        scratch_shapes=[
            pltpu.VMEM((TOK, D), BF16),
            pltpu.VMEM((TOK, 1), F32),
            pltpu.VMEM((TOK, ROWS), F32),
            pltpu.VMEM((16, TOK, ROWS), BF16),
            pltpu.VMEM((NY, GROUP, ROWS), BF16),
            pltpu.VMEM((GROUP, KV), BF16),
            pltpu.VMEM((NY, ROWS, KV), BF16),
            pltpu.VMEM((NY, GROUP, ROWS), BF16),
            pltpu.VMEM((16, TOK, ROWS), BF16),
            pltpu.VMEM((GROUP, KV), F32),
            pltpu.VMEM((GROUP, KV), BF16),
            pltpu.VMEM((2, TOK // 2, KV), BF16),
            pltpu.VMEM((2, TOK, KV), BF16),
            pltpu.VMEM((NY, ROWS, KV), F32),
            pltpu.VMEM((NY, ROWS, KV), BF16),
            pltpu.VMEM((5, ROWS, KV), BF16),
            pltpu.VMEM((TOK, KV), BF16),
            pltpu.VMEM((TOK, KV), BF16),
            pltpu.VMEM((TOK, KV), BF16),
            pltpu.VMEM((TOK, KV), BF16),
            pltpu.VMEM((TOK, KV), BF16),
            pltpu.VMEM((NZ - 1, SLICE, KV), BF16),
            pltpu.VMEM((2, TOK, KV), BF16),
            pltpu.VMEM((ROWS, KV), F32),
            dma((5,)),
            dma((NX,)), dma((NX,)),
            dma((NY, NX)), dma((NY, NX)),
            dma((NY, NX)), dma((NY, NX)),
            dma((NX,)), dma((NX,)),
            dma((5, 2)), dma((NY, 2)),
            dma((5,)), dma((5,)),
            dma((3,)), dma((3,)),
            dma((NZ,)), dma((NZ,)),
            dma((NZ,)), dma((NZ,)),
            pltpu.SemaphoreType.REGULAR,
            pltpu.SemaphoreType.REGULAR,
        ],
        compiler_params=pltpu.CompilerParams(
            collective_id=0, has_side_effects=True, vmem_limit_bytes=40 * 1024 * 1024
        ),
    )(*[pltpu.with_memory_space_constraint(a, pltpu.HBM) for a in (hidden[0], gain, value_grad[0], value_weight[0], outer_delta[0], momentum)])
    hidden_grad, values, weight_grad, new_momentum, outer_step = pl.pallas_call(
        store,
        out_shape=shapes,
        in_specs=[anywhere] * 5,
        out_specs=[anywhere] * 5,
        scratch_shapes=[dma((5,))],
        compiler_params=pltpu.CompilerParams(vmem_limit_bytes=1024 * 1024),
    )(*outs)
    return (values[None], weight_grad[None], hidden_grad[None], new_momentum, outer_step)


def solution(mesh):
    in_specs = (
        P("rep", "fsdp", None),
        P("rep", None),
        P("rep", "fsdp", None),
        P("rep", "fsdp", None),
        P("rep", "fsdp", None),
        P("fsdp", None),
    )
    out_specs = (
        P("rep", "fsdp", None),
        P("rep", "fsdp", None),
        P("rep", "fsdp", None),
        P("fsdp", None),
        P("fsdp", None),
    )
    return jax.shard_map(
        per_device, mesh=mesh, in_specs=in_specs, out_specs=out_specs, check_vma=False
    )
```

```python
import jax
import jax.numpy as jnp
from jax import lax
from jax.experimental import pallas as pl
from jax.experimental.pallas import tpu as pltpu
from jax.sharding import PartitionSpec as P

EPSILON = 1e-05
MOMENT = 0.9
OUTER_RATE = 0.7

TOK = 128
D = 4096
KV = 512
ROWS = 256
NX = 4
NY = 4
NZ = 8
GROUP = NX * TOK
SLICE = 16

MESH = pl.DeviceIdType.MESH
F32 = jnp.float32
BF16 = jnp.bfloat16


def exchange(
    hidden, gain, value_grad, weight, delta, momentum,
    hg_out, val_out, wg_out, nm_out, os_out,
    h_v, inv_v, row_v, n_send, n_buf, vg_buf, w_buf, ng_send, ng_buf,
    v_part, v_send, v_mid, v_recv, wg_acc, wg_send, wg_recv,
    d_own, d_recv, q_send, q_recv, p_send, z_recv, avg, mom_v,
    local_sem, x_send, x_recv, n_ssem, n_rsem, g_ssem, g_rsem, v_ssem, v_rsem,
    w_ssem, w_rsem, r_ssem, r_rsem, c_ssem, c_rsem, z_ssem, z_rsem, a_ssem, a_rsem,
    below_sem, above_sem,
):
    rep = lax.axis_index("rep")
    fsdp = lax.axis_index("fsdp")
    i, j = fsdp // NY, fsdp % NY
    z, core = rep // 4, rep % 2
    high = j // 2
    mid = jnp.logical_or(j == 1, j == 2)
    outer = jnp.logical_not(mid)
    is_mid = high + j % 2 - 2 * high * (j % 2)

    def along_x(d):
        return (rep, ((i + d) % NX) * NY + j)

    def along_z(d):
        return (((z + d) % NZ) * 4 + rep % 4, fsdp)

    inward = (rep, i * NY + j + 1 - 2 * high)
    outward = (rep, i * NY + j - 1 + 2 * high)
    other_core = (rep + 1 - 2 * core, fsdp)
    other_half = (rep + 2 - 4 * ((rep // 2) % 2), fsdp)
    near = j + 1 - 2 * (j % 2)
    far_mid = 2 - high
    far_outer = 3 - 3 * high
    arrival = (j, near, far_mid, far_outer)
    order = (far_outer, far_mid, near, j)

    def remote(src, dst, ssem, rsem, device):
        return pltpu.make_async_remote_copy(
            src_ref=src, dst_ref=dst, send_sem=ssem, recv_sem=rsem,
            device_id=device, device_id_type=MESH,
        )

    barrier = pltpu.get_barrier_semaphore()

    def greet(device):
        pl.semaphore_signal(barrier, inc=1, device_id=device, device_id_type=MESH)

    for d in range(1, NX):
        greet(along_x(d))
    greet(inward)

    @pl.when(mid)
    def _():
        greet(outward)

    greet(other_core)
    late = z >= NZ // 2

    greet(other_half)
    for d in range(1, NZ):
        there = (z + d) % NZ
        both_late = jnp.logical_and(late, there >= NZ // 2)
        beside = jnp.logical_or(there == z + 1, there == z - 1)

        @pl.when(jnp.logical_or(both_late, beside))
        def _():
            greet(along_z(d))

    own_rows = pl.ds(pl.multiple_of(i * TOK, TOK), TOK)
    half_rows = lambda h: pl.ds(pl.multiple_of(h * TOK, TOK), TOK)
    slice_rows = lambda s: pl.ds(pl.multiple_of(s * SLICE, SLICE), SLICE)

    loads = [
        pltpu.make_async_copy(hidden, h_v, local_sem.at[0]),
        pltpu.make_async_copy(value_grad, vg_buf.at[own_rows], local_sem.at[1]),
        pltpu.make_async_copy(weight, w_buf.at[j], local_sem.at[2]),
        pltpu.make_async_copy(delta.at[half_rows(core)], d_own, local_sem.at[3]),
        pltpu.make_async_copy(momentum, mom_v, local_sem.at[4]),
    ]
    for load in loads:
        load.start()

    upper = z // 4
    first, fifth = 1 - (z + 7) // 8, upper * (1 - (z + 3) // 8)
    z_greeted = (1 - upper) * (2 - first) + upper * (3 + fifth)
    pl.semaphore_wait(barrier, 6 + is_mid + z_greeted)

    vg_first = [
        remote(value_grad, vg_buf.at[own_rows], x_send.at[d], x_recv.at[d], along_x(d))
        for d in (1, 3)
    ]
    for copy in vg_first:
        copy.start()
    half_tok = TOK // 2

    def part_rows(d, h):
        return pl.ds(pl.multiple_of(((i + d) % NX) * TOK + h * half_tok, half_tok), half_tok)

    vg_second = [
        remote(
            vg_buf.at[part_rows(NX - d, h)], vg_buf.at[part_rows(NX - d, h)],
            x_send.at[2 * h], x_recv.at[2 * h], along_x(d),
        )
        for d, h in ((1, 0), (3, 1))
    ]
    def w_half(h):
        return pl.ds(h * (ROWS // 2), ROWS // 2)

    def w_own(h, way, device):
        return remote(
            weight.at[w_half(h)], w_buf.at[j, w_half(h)],
            w_ssem.at[way, h], w_rsem.at[j, h], device,
        )

    for h in range(2):
        w_own(h, 0, inward).start()

        @pl.when(mid)
        def _():
            w_own(h, 1, outward).start()

    core_half = remote(
        delta.at[half_rows(1 - core)], d_recv, c_ssem.at[0], c_rsem.at[0], other_core
    )
    core_half.start()

    def tell(semaphore, device):
        pl.semaphore_signal(semaphore, inc=1, device_id=device, device_id_type=MESH)

    @pl.when(jnp.logical_and(z > 0, z <= 4))
    def _():
        pl.semaphore_wait(below_sem, 1)

    @pl.when(z < 4)
    def _():
        tell(below_sem, along_z(1))

    @pl.when(z == 4)
    def _():
        for d in range(1, 4):
            tell(below_sem, along_z(d))

    loads[0].wait()

    def columns(f):
        return pl.ds(pl.multiple_of(f * ROWS, ROWS), ROWS)

    def add_square(f, total):
        block = h_v[:, columns(f)].astype(F32)
        return total + block * block

    squares = lax.fori_loop(0, 16, add_square, jnp.zeros((TOK, ROWS), F32))
    inv_v[...] = lax.rsqrt(jnp.sum(squares, axis=-1, keepdims=True) / D + EPSILON)

    def make_normed(block):
        @pl.loop(0, NX)
        def _(part):
            f = part * NY + block
            scaled = h_v[:, columns(f)].astype(F32) * inv_v[...]
            n_send[f] = (scaled * gain[:, columns(f)].astype(F32)).astype(BF16)

    def spread_word():
        @pl.when(z > 4)
        def _():
            pl.semaphore_wait(below_sem, 1)

        for d in range(2, NZ):
            @pl.when(jnp.logical_and(z >= d, z < d + 4))
            def _():
                tell(above_sem, along_z(NZ - d))

        loads[3].wait()
        core_half.wait_recv()
        q_send[...] = (d_own[...].astype(F32) + d_recv[...].astype(F32)).astype(BF16)
        half_copy = remote(q_send, q_recv, c_ssem.at[1], c_rsem.at[1], other_half)
        half_copy.start()
        return half_copy

    n_copies = []
    for n, block in enumerate(order):
        make_normed(block)
        for d in (1, 3, 2):
            copy = remote(
                n_send.at[((i + d) % NX) * NY + block], n_buf.at[block, own_rows],
                n_ssem.at[n, d], n_rsem.at[n, d], along_x(d),
            )
            copy.start()
            n_copies.append(copy)
        if n == 0:
            half_copy = spread_word()
            for first, second in zip(vg_first, vg_second):
                first.wait_recv()
                second.start()
    for block in range(NY):
        n_buf[block, own_rows] = n_send[i * NY + block]

    z_copies = [
        remote(
            p_send.at[slice_rows((z + d) % NZ)], z_recv.at[d - 1],
            z_ssem.at[d], z_rsem.at[d], along_z(d),
        )
        for d in range(1, NZ)
    ]

    def send_slices():
        half_copy.wait_recv()
        p_send[...] = (q_send[...].astype(F32) + q_recv[...].astype(F32)).astype(BF16)

        @pl.when(z < 4)
        def _():
            pl.semaphore_wait(above_sem, 6 - z)

        for copy in z_copies:
            copy.start()

    a_copies = [
        remote(
            avg.at[core, slice_rows(z)], avg.at[core, slice_rows(z)],
            a_ssem.at[d], a_rsem.at[d], along_z(d),
        )
        for d in range(1, NZ)
    ]

    def send_average():
        for copy in z_copies:
            copy.wait_recv()
        total = q_send[slice_rows(z)].astype(F32) + q_recv[slice_rows(z)].astype(F32)
        for d in range(NZ - 1):
            total = total + z_recv[d].astype(F32)
        avg[core, slice_rows(z)] = (total / 32.0).astype(BF16)
        for copy in a_copies:
            copy.start()

    core_full = remote(avg.at[core], avg.at[core], c_ssem.at[2], c_rsem.at[2], other_core)
    core_back = remote(
        avg.at[1 - core], avg.at[1 - core], c_ssem.at[2], c_rsem.at[2], other_core
    )

    def share_average():
        for copy in a_copies:
            copy.wait_recv()
        core_full.start()

    def w_forward(n, h):
        part = w_buf.at[arrival[n], w_half(h)]
        return remote(
            part, part, w_ssem.at[n + 1, h], w_rsem.at[arrival[n], h],
            inward if n == 1 else outward,
        )

    def forward_weight(n, h):
        @pl.when(mid)
        def _():
            w_forward(n, h).wait_recv()
            w_forward(n, h).start()

    def await_weight(n):
        @pl.when(outer)
        def _():
            for h in range(2):
                w_forward(n, h).wait_recv()

    g_copies = []

    def send_grad(n):
        block = arrival[n]
        ng_send[n] = lax.dot_general(
            vg_buf[...], w_buf[block], (((1,), (1,)), ((), ())), preferred_element_type=F32
        ).astype(BF16)
        for d in (1, 3, 2):
            copy = remote(
                ng_send.at[n, pl.ds(pl.multiple_of(((i + d) % NX) * TOK, TOK), TOK)],
                ng_buf.at[i * NY + block], g_ssem.at[n, d], g_rsem.at[n, d], along_x(d),
            )
            copy.start()
            g_copies.append(copy)
        ng_buf[i * NY + block] = ng_send[n, own_rows]

    def make_weight_grad(n):
        for d in range(1, NX):
            n_copies[3 * n + (0, 0, 2, 1)[d]].wait_recv()
        block = order[n]
        wg_acc[block] = lax.dot_general(
            n_buf[block], vg_buf[...], (((0,), (0,)), ((), ())), preferred_element_type=F32
        ) * (1.0 / TOK)

    def first_hop(n):
        return remote(
            wg_send.at[order[n]], wg_recv.at[n], r_ssem.at[n], r_rsem.at[n], inward
        )

    def start_chain(n):
        @pl.when(outer)
        def _():
            wg_send[order[n]] = wg_acc[order[n]].astype(BF16)
            first_hop(n).start()

    def next_hop(slot):
        block, target, device = (
            (far_outer, 3, inward), (far_mid, 4, inward), None, (near, 3, outward),
        )[slot]
        return block, remote(
            wg_send.at[block], wg_recv.at[target], r_ssem.at[slot], r_rsem.at[target], device
        )

    def r_arrive(slot):
        remote(
            wg_recv.at[slot], wg_recv.at[slot], r_ssem.at[0], r_rsem.at[slot], inward
        ).wait_recv()

    def pass_on(slot):
        @pl.when(mid)
        def _():
            block, copy = next_hop(slot)
            r_arrive(slot)
            wg_send[block] = (wg_acc[block] + wg_recv[slot].astype(F32)).astype(BF16)
            copy.start()

    for h in range(2):
        forward_weight(1, h)
        forward_weight(2, h)
    loads[1].wait()
    loads[2].wait()
    for copy in vg_second:
        copy.wait_recv()
    send_grad(0)
    forward_weight(3, 0)
    await_weight(1)
    make_weight_grad(0)
    start_chain(0)
    pl.when(late)(send_slices)
    send_grad(1)
    forward_weight(3, 1)
    make_weight_grad(1)
    start_chain(1)
    pl.when(jnp.logical_not(late))(send_slices)
    await_weight(2)
    send_grad(2)
    make_weight_grad(2)
    start_chain(2)
    pass_on(0)
    pl.when(late)(send_average)
    make_weight_grad(3)
    await_weight(3)

    v_acc = jnp.dot(n_buf[0], w_buf[0], preferred_element_type=F32)
    for block in range(1, NY):
        v_acc = v_acc + jnp.dot(n_buf[block], w_buf[block], preferred_element_type=F32)
    v_part[...] = v_acc
    v_copies = []
    for d, h in ((1, 0), (3, 1)):
        rows = part_rows(2, h)
        v_send[rows] = v_part[rows].astype(BF16)
        copy = remote(v_send.at[rows], v_mid.at[h], v_ssem.at[h], v_rsem.at[h], along_x(d))
        copy.start()
        v_copies.append(copy)
    send_grad(3)
    pl.when(jnp.logical_not(late))(send_average)

    def send_values():
        for d, h in ((1, 0), (3, 1)):
            v_copies[h].wait_recv()
            added, kept = part_rows(d, h), part_rows(d, 1 - h)
            v_send[added] = (v_part[added] + v_mid[h].astype(F32)).astype(BF16)
            v_send[kept] = v_part[kept].astype(BF16)
            rows = pl.ds(pl.multiple_of(((i + d) % NX) * TOK, TOK), TOK)
            copy = remote(
                v_send.at[rows], v_recv.at[h], v_ssem.at[2 + h], v_rsem.at[2 + h], along_x(d)
            )
            copy.start()
            v_copies.append(copy)

    def gated_scaled(f):
        scaled = h_v[:, columns(f)].astype(F32) * inv_v[...]
        gated = ng_buf[f].astype(F32) * gain[:, columns(f)].astype(F32)
        return gated, scaled

    row_v[...] = jnp.zeros_like(row_v)

    def add_rows(f):
        gated, scaled = gated_scaled(f)
        row_v[...] += gated * scaled

    def take_grad(n):
        add_rows(i * NY + arrival[n])
        for d in range(1, NX):
            g_copies[3 * n + (0, 0, 2, 1)[d]].wait_recv()
            add_rows(((i + NX - d) % NX) * NY + arrival[n])

    pass_on(1)
    pass_on(3)
    take_grad(0)
    take_grad(1)
    take_grad(2)
    send_values()
    share_average()
    take_grad(3)
    mean = jnp.sum(row_v[...], axis=-1, keepdims=True) / D

    @pl.loop(0, 16)
    def _(f):
        gated, scaled = gated_scaled(f)
        hg_out[:, columns(f)] = (inv_v[...] * (gated - scaled * mean)).astype(BF16)

    @pl.when(outer)
    def _():
        r_arrive(3)
        wg_out[...] = (wg_acc[j] + wg_recv[3].astype(F32)).astype(BF16)

    @pl.when(mid)
    def _():
        r_arrive(2)
        r_arrive(4)
        wg_out[...] = (
            wg_acc[j] + wg_recv[2].astype(F32) + wg_recv[4].astype(F32)
        ).astype(BF16)

    core_back.wait_recv()
    loads[4].wait()
    for h in range(2):
        rows = pl.ds(h * TOK, TOK)
        average = avg[h].astype(F32)
        new_momentum = MOMENT * mom_v[rows] + average
        nm_out[rows] = new_momentum
        os_out[rows] = -OUTER_RATE * (average + MOMENT * new_momentum)

    value_sum = v_part[own_rows]
    for h in range(2):
        v_copies[2 + h].wait_recv()
        value_sum = value_sum + v_recv[h].astype(F32)
    val_out[...] = value_sum.astype(BF16)

    for copy in (*vg_first, *vg_second, w_own(0, 0, inward), w_own(1, 0, inward), core_half, *n_copies, *z_copies, *g_copies, *a_copies):
        copy.wait_send()
    for copy in (*v_copies, core_full, half_copy):
        copy.wait_send()

    @pl.when(mid)
    def _():
        for h in range(2):
            w_own(h, 1, outward).wait_send()
            for n in range(1, NY):
                w_forward(n, h).wait_send()
        for slot in (0, 1, 3):
            next_hop(slot)[1].wait_send()

    @pl.when(outer)
    def _():
        for n in range(3):
            first_hop(n).wait_send()


def store(*refs):
    sems = refs[-1]
    copies = [
        pltpu.make_async_copy(refs[k], refs[5 + k], sems.at[k]) for k in range(5)
    ]
    for copy in copies:
        copy.start()
    for copy in copies:
        copy.wait()


def per_device(hidden, gain, value_grad, value_weight, outer_delta, momentum):
    anywhere = pl.BlockSpec(memory_space=pl.ANY)
    vmem = pl.BlockSpec(memory_space=pltpu.VMEM)
    dma = pltpu.SemaphoreType.DMA
    shapes = (
        jax.ShapeDtypeStruct((TOK, D), BF16),
        jax.ShapeDtypeStruct((TOK, KV), BF16),
        jax.ShapeDtypeStruct((ROWS, KV), BF16),
        jax.ShapeDtypeStruct((ROWS, KV), F32),
        jax.ShapeDtypeStruct((ROWS, KV), F32),
    )
    outs = pl.pallas_call(
        exchange,
        out_shape=shapes,
        in_specs=[anywhere, vmem, anywhere, anywhere, anywhere, anywhere],
        out_specs=[vmem] * 5,
        scratch_shapes=[
            pltpu.VMEM((TOK, D), BF16),
            pltpu.VMEM((TOK, 1), F32),
            pltpu.VMEM((TOK, ROWS), F32),
            pltpu.VMEM((16, TOK, ROWS), BF16),
            pltpu.VMEM((NY, GROUP, ROWS), BF16),
            pltpu.VMEM((GROUP, KV), BF16),
            pltpu.VMEM((NY, ROWS, KV), BF16),
            pltpu.VMEM((NY, GROUP, ROWS), BF16),
            pltpu.VMEM((16, TOK, ROWS), BF16),
            pltpu.VMEM((GROUP, KV), F32),
            pltpu.VMEM((GROUP, KV), BF16),
            pltpu.VMEM((2, TOK // 2, KV), BF16),
            pltpu.VMEM((2, TOK, KV), BF16),
            pltpu.VMEM((NY, ROWS, KV), F32),
            pltpu.VMEM((NY, ROWS, KV), BF16),
            pltpu.VMEM((5, ROWS, KV), BF16),
            pltpu.VMEM((TOK, KV), BF16),
            pltpu.VMEM((TOK, KV), BF16),
            pltpu.VMEM((TOK, KV), BF16),
            pltpu.VMEM((TOK, KV), BF16),
            pltpu.VMEM((TOK, KV), BF16),
            pltpu.VMEM((NZ - 1, SLICE, KV), BF16),
            pltpu.VMEM((2, TOK, KV), BF16),
            pltpu.VMEM((ROWS, KV), F32),
            dma((5,)),
            dma((NX,)), dma((NX,)),
            dma((NY, NX)), dma((NY, NX)),
            dma((NY, NX)), dma((NY, NX)),
            dma((NX,)), dma((NX,)),
            dma((5, 2)), dma((NY, 2)),
            dma((5,)), dma((5,)),
            dma((3,)), dma((3,)),
            dma((NZ,)), dma((NZ,)),
            dma((NZ,)), dma((NZ,)),
            pltpu.SemaphoreType.REGULAR,
            pltpu.SemaphoreType.REGULAR,
        ],
        compiler_params=pltpu.CompilerParams(
            collective_id=0, has_side_effects=True, vmem_limit_bytes=40 * 1024 * 1024
        ),
    )(*[pltpu.with_memory_space_constraint(a, pltpu.HBM) for a in (hidden[0], gain, value_grad[0], value_weight[0], outer_delta[0], momentum)])
    hidden_grad, values, weight_grad, new_momentum, outer_step = pl.pallas_call(
        store,
        out_shape=shapes,
        in_specs=[anywhere] * 5,
        out_specs=[anywhere] * 5,
        scratch_shapes=[dma((5,))],
        compiler_params=pltpu.CompilerParams(vmem_limit_bytes=1024 * 1024),
    )(*outs)
    return (values[None], weight_grad[None], hidden_grad[None], new_momentum, outer_step)


def solution(mesh):
    in_specs = (
        P("rep", "fsdp", None),
        P("rep", None),
        P("rep", "fsdp", None),
        P("rep", "fsdp", None),
        P("rep", "fsdp", None),
        P("fsdp", None),
    )
    out_specs = (
        P("rep", "fsdp", None),
        P("rep", "fsdp", None),
        P("rep", "fsdp", None),
        P("fsdp", None),
        P("fsdp", None),
    )
    return jax.shard_map(
        per_device, mesh=mesh, in_specs=in_specs, out_specs=out_specs, check_vma=False
    )
```
